256 devices in a mesh: depth: 16 (over y_lo, x, core), cols: 16 (over z, y_hi).
Axes of the slice: x: 4, y: 4 (y_hi: 2, y_lo: 2; y = y_hi * 2 + y_lo), z: 8, core: 2. Of those that a mesh axis runs over, the one named last changes fastest.
Arguments:
- alignment_activations: bfloat16 [256, 512, 768], P('depth', 'cols'), may hold values from -6 to 6
- occupancy_indicator: int32 [256, 512], P('depth', 'cols'), may hold values from 0 to 1, as said below
- horizontal_probe_proj: bfloat16 [768, 768], replicated
- horizontal_lookup_proj: bfloat16 [768, 768], replicated
- horizontal_content_proj: bfloat16 [768, 768], replicated, may hold values from -0.21875 to 0.21875
- horizontal_result_proj: bfloat16 [768, 768], replicated, may hold values from -0.21875 to 0.21875
- vertical_probe_proj: bfloat16 [768, 768], replicated
- vertical_lookup_proj: bfloat16 [768, 768], replicated
- vertical_content_proj: bfloat16 [768, 768], replicated, may hold values from -0.21875 to 0.21875
- vertical_result_proj: bfloat16 [768, 768], replicated, may hold values from -0.21875 to 0.21875
- pairing_first_factor: bfloat16 [768, 32], replicated, may hold values from -0.21875 to 0.21875
- pairing_second_factor: bfloat16 [768, 32], replicated, may hold values from -0.21875 to 0.21875
- pairing_channel_proj: bfloat16 [1024, 128], replicated, may hold values from -4 to 4
Outputs:
- alignment_output: bfloat16 [256, 512, 768], P('depth', 'cols')
- pair: bfloat16 [512, 512, 128], P('cols', 'depth')
The draws below stay inside these ranges and needn't reach their ends.
Inputs may be any that keep to these rules, and one draw needn't show every extreme that they name: `occupancy_indicator`: sequence 0 has no padding; every other sequence has residues on the columns from 0 up to some last column, more than 384 columns in all, and padding after it.
All inputs are finite; a program needn't handle non-finite values.
Results may differ from the reference program's by a relative error of at most 0.028.
Values may be sent and summed in bfloat16 or wider, within the bound.
No kernel may reach another device: no remote copies, remote signals or barrier semaphores. Data moves between devices by JAX's collectives and lax.ppermute only.
A program may use at most 128 MiB of HBM per device.

```python
import math
import jax
import jax.numpy as jnp
from jax import lax

EMBED_DIMENSION = 768
H = 12
HD = 64
C = 32
P_SIZE = 128
HOMOLOG_TOTAL = 256
SITE_TOTAL = 512


def paired(key, tag):
    return jax.random.normal(jax.random.fold_in(key, tag), (EMBED_DIMENSION, EMBED_DIMENSION), jnp.float32)


def draw_occupancy_indicator(key, part):
    key = jax.random.fold_in(key, 5)
    last = SITE_TOTAL - jax.random.randint(key, (HOMOLOG_TOTAL, 1), 0, SITE_TOTAL // 4)
    seq_ids = jnp.arange(HOMOLOG_TOTAL, dtype=jnp.int32)[:, None]
    last = jnp.where(seq_ids == 0, SITE_TOTAL, last)
    positions = jnp.arange(SITE_TOTAL, dtype=jnp.int32)[None, :]
    return (positions < last).astype(jnp.int32)


def draw_horizontal_lookup_proj(key, part):
    base = paired(key, 11)
    key = jax.random.fold_in(key, 31)
    noise = jax.random.normal(key, (EMBED_DIMENSION, EMBED_DIMENSION), jnp.float32)
    return (2.0 * (base + 0.3 * noise) * EMBED_DIMENSION ** (-0.5)).astype(jnp.bfloat16)


def draw_horizontal_probe_proj(key, part):
    key = jax.random.fold_in(key, 32)
    weight = 2.0 * jax.random.normal(key, (EMBED_DIMENSION, EMBED_DIMENSION), jnp.float32) * EMBED_DIMENSION ** (-0.5)
    return weight.astype(jnp.bfloat16)


def draw_vertical_lookup_proj(key, part):
    base = paired(key, 12)
    key = jax.random.fold_in(key, 33)
    noise = jax.random.normal(key, (EMBED_DIMENSION, EMBED_DIMENSION), jnp.float32)
    return ((base + 0.3 * noise) * EMBED_DIMENSION ** (-0.5)).astype(jnp.bfloat16)


def draw_vertical_probe_proj(key, part):
    key = jax.random.fold_in(key, 34)
    weight = jax.random.normal(key, (EMBED_DIMENSION, EMBED_DIMENSION), jnp.float32) * EMBED_DIMENSION ** (-0.5)
    return weight.astype(jnp.bfloat16)


def levels(stream_key, extent, shards, low, top_value):
    def one(axis_at, parts):
        draws = jax.random.uniform(jax.random.fold_in(jax.random.fold_in(stream_key, 6), axis_at), (parts,), jnp.float32, low / len(shards), top_value / len(shards))
        return jnp.repeat(jnp.exp(draws), extent[axis_at] // parts).reshape((-1,) + (1,) * (len(extent) - axis_at - 1))

    gain = one(*shards[0])
    for cut in shards[1:]:
        gain = gain * one(*cut)
    return gain


def gaussian(key, dims, deviation, most, split=(), kind=jnp.bfloat16):
    factor_of = levels(key, dims, split, -0.22, 0.18) if split else 1.0
    drawn = jax.random.normal(key, dims, jnp.float32) * deviation * factor_of
    return jnp.minimum(jnp.maximum(drawn, -most), most).astype(kind)


def setup_inputs(seed: int = 0) -> dict:
    streams_of = jax.random.split(jax.random.key(seed), 14)
    alignment_activations = gaussian(streams_of[0], (HOMOLOG_TOTAL, SITE_TOTAL, EMBED_DIMENSION), 1.0, 6.0, ((0, 16), (1, 16)))
    occupancy_indicator = draw_occupancy_indicator(jax.random.fold_in(streams_of[13], 71), 0)
    horizontal_probe_proj = draw_horizontal_probe_proj(jax.random.fold_in(streams_of[13], 71), 0)
    horizontal_lookup_proj = draw_horizontal_lookup_proj(jax.random.fold_in(streams_of[13], 71), 0)
    horizontal_content_proj = gaussian(streams_of[4], (EMBED_DIMENSION, EMBED_DIMENSION), EMBED_DIMENSION ** -0.5, 0.21875)
    horizontal_result_proj = gaussian(streams_of[5], (EMBED_DIMENSION, EMBED_DIMENSION), EMBED_DIMENSION ** -0.5, 0.21875)
    vertical_probe_proj = draw_vertical_probe_proj(jax.random.fold_in(streams_of[13], 71), 0)
    vertical_lookup_proj = draw_vertical_lookup_proj(jax.random.fold_in(streams_of[13], 71), 0)
    vertical_content_proj = gaussian(streams_of[8], (EMBED_DIMENSION, EMBED_DIMENSION), EMBED_DIMENSION ** -0.5, 0.21875)
    vertical_result_proj = gaussian(streams_of[9], (EMBED_DIMENSION, EMBED_DIMENSION), EMBED_DIMENSION ** -0.5, 0.21875)
    pairing_first_factor = gaussian(streams_of[10], (EMBED_DIMENSION, C), EMBED_DIMENSION ** -0.5, 0.21875)
    pairing_second_factor = gaussian(streams_of[11], (EMBED_DIMENSION, C), EMBED_DIMENSION ** -0.5, 0.21875)
    pairing_channel_proj = gaussian(streams_of[12], (C * C, P_SIZE), 0.3, 4.0)
    return {"alignment_activations": alignment_activations, "occupancy_indicator": occupancy_indicator, "horizontal_probe_proj": horizontal_probe_proj, "horizontal_lookup_proj": horizontal_lookup_proj, "horizontal_content_proj": horizontal_content_proj, "horizontal_result_proj": horizontal_result_proj, "vertical_probe_proj": vertical_probe_proj, "vertical_lookup_proj": vertical_lookup_proj, "vertical_content_proj": vertical_content_proj, "vertical_result_proj": vertical_result_proj, "pairing_first_factor": pairing_first_factor, "pairing_second_factor": pairing_second_factor, "pairing_channel_proj": pairing_channel_proj}


def standardize_features(values):
    wide = values.astype(jnp.float32)
    center = wide - lax.optimization_barrier(jnp.mean(wide, axis=-1, keepdims=True))
    spread = lax.optimization_barrier(jnp.mean(center * center, axis=-1, keepdims=True))
    return (center * lax.rsqrt(spread + 1e-05)).astype(jnp.bfloat16)

def project_through(values, weight):
    return jnp.dot(values, weight, preferred_element_type=jnp.float32)

def reference(alignment_activations, occupancy_indicator, horizontal_probe_proj, horizontal_lookup_proj, horizontal_content_proj, horizontal_result_proj, vertical_probe_proj, vertical_lookup_proj, vertical_content_proj, vertical_result_proj, pairing_first_factor, pairing_second_factor, pairing_channel_proj):
    portion_beginning = alignment_activations
    live = occupancy_indicator.astype(jnp.float32)
    standardized_features = standardize_features(portion_beginning)
    query = (project_through(standardized_features, horizontal_probe_proj) * live[:, :, None]).astype(jnp.bfloat16)
    keys = (project_through(standardized_features, horizontal_lookup_proj) * live[:, :, None]).astype(jnp.bfloat16)
    values = project_through(standardized_features, horizontal_content_proj).astype(jnp.bfloat16)
    query_heads = query.astype(jnp.float32).reshape(HOMOLOG_TOTAL, SITE_TOTAL, H, HD)
    key_heads = keys.astype(jnp.float32).reshape(HOMOLOG_TOTAL, SITE_TOTAL, H, HD)
    value_heads = values.astype(jnp.float32).reshape(HOMOLOG_TOTAL, SITE_TOTAL, H, HD)
    tied = jnp.einsum('sihe,sjhe->ihj', query_heads, key_heads) * (1.0 / math.sqrt(HD * HOMOLOG_TOTAL))
    row_p = jax.nn.softmax(tied, axis=-1).astype(jnp.bfloat16)
    row_mix = jnp.einsum('ihj,sjhe->sihe', row_p.astype(jnp.float32), value_heads).astype(jnp.bfloat16).reshape(HOMOLOG_TOTAL, SITE_TOTAL, EMBED_DIMENSION)
    state_after_row_attention = (portion_beginning.astype(jnp.float32) + project_through(row_mix, horizontal_result_proj)).astype(jnp.bfloat16)
    standardized_features = standardize_features(state_after_row_attention)

    def one_column(pieces):
        column, alive = pieces
        col_q = project_through(column, vertical_probe_proj).astype(jnp.bfloat16).astype(jnp.float32).reshape(HOMOLOG_TOTAL, H, HD)
        col_k = project_through(column, vertical_lookup_proj).astype(jnp.bfloat16).astype(jnp.float32).reshape(HOMOLOG_TOTAL, H, HD)
        col_v = project_through(column, vertical_content_proj).astype(jnp.bfloat16).astype(jnp.float32).reshape(HOMOLOG_TOTAL, H, HD)
        logits = jnp.einsum('she,the->hst', col_q, col_k) * (1.0 / math.sqrt(HD))
        logits = jnp.where(alive[None, None, :] > 0, logits, -1000000000.0)
        col_p = jax.nn.softmax(logits, axis=-1).astype(jnp.bfloat16)
        return jnp.einsum('hst,the->she', col_p.astype(jnp.float32), col_v).astype(jnp.bfloat16).reshape(HOMOLOG_TOTAL, EMBED_DIMENSION)
    column_mixing = lax.map(one_column, (jnp.swapaxes(standardized_features, 0, 1), jnp.swapaxes(live, 0, 1)))
    column_mixing = jnp.swapaxes(column_mixing, 0, 1)
    alignment_output = (state_after_row_attention.astype(jnp.float32) + project_through(column_mixing, vertical_result_proj)).astype(jnp.bfloat16)
    standardized_features = standardize_features(alignment_output)
    left = (project_through(standardized_features, pairing_first_factor) * live[:, :, None]).astype(jnp.bfloat16).astype(jnp.float32)
    right = (project_through(standardized_features, pairing_second_factor) * live[:, :, None]).astype(jnp.bfloat16).astype(jnp.float32)
    count = jnp.dot(live.T, live, preferred_element_type=jnp.float32)
    block = 16

    def pair_rows(first):
        part = lax.dynamic_slice_in_dim(left, first, block, 1)
        outer = jnp.einsum('sic,sje->ijce', part, right).astype(jnp.bfloat16)
        projected = jnp.dot(outer.reshape(block, SITE_TOTAL, C * C), pairing_channel_proj, preferred_element_type=jnp.float32)
        counted = lax.dynamic_slice_in_dim(count, first, block, 0)
        return (projected / (counted[:, :, None] + 0.001)).astype(jnp.bfloat16)
    pair = lax.map(pair_rows, jnp.arange(0, SITE_TOTAL, block, dtype=jnp.int32)).reshape(SITE_TOTAL, SITE_TOTAL, P_SIZE)
    return (alignment_output, pair)
```

```python
import functools
import math

import jax
import jax.numpy as jnp
from jax import lax
from jax.experimental import pallas as pl
from jax.experimental.pallas import tpu as pltpu
from jax.sharding import PartitionSpec as P

f32 = jnp.float32
bf16 = jnp.bfloat16

S = 16
I = 32
E = 768
H = 12
N = 16
ROWS = S * I
SEQS = 256
SITES = 512
C = 32
PC = 128
LR = 80
VMEM = 60 * 1024 * 1024

NT = (((1,), (1,)), ((), ()))


def norm(wide):
    center = wide - jnp.mean(wide, axis=-1, keepdims=True)
    spread = jnp.mean(center * center, axis=-1, keepdims=True)
    return (center * lax.rsqrt(spread + 1e-05)).astype(bf16)


def mm(a, b):
    return jnp.dot(a, b, preferred_element_type=f32)


def mmt(a, b):
    return lax.dot_general(a, b, NT, preferred_element_type=f32)


def lanes_lo(a, b):
    return jnp.concatenate([a[:, :64], b[:, :64]], axis=1)


def lanes_hi(a, b):
    return jnp.concatenate([a[:, 64:], b[:, 64:]], axis=1)


def whole(n):
    return [pl.BlockSpec(memory_space=pltpu.VMEM)] * n


def params(**kw):
    return pltpu.CompilerParams(vmem_limit_bytes=VMEM, **kw)


def cost(flops, bytes_accessed, transcendentals=0):
    return pl.CostEstimate(
        flops=flops, bytes_accessed=bytes_accessed, transcendentals=transcendentals
    )


def row_proj_kernel(x_ref, live_ref, wq_ref, wk_ref, wv_ref, qk_ref, v_ref, xn_ref):
    @pl.when(pl.program_id(0) == 0)
    def _():
        xn_ref[...] = norm(x_ref[...].astype(f32))

    xn = xn_ref[...]
    live = live_ref[...]
    half = ROWS // 2

    def put(ref, w_ref, index, masked):
        y = mm(xn, w_ref[...])
        if masked:
            y = y * live
        y = y.astype(bf16)
        for t in range(2):
            a = y[:half, 128 * t : 128 * t + 128]
            b = y[half:, 128 * t : 128 * t + 128]
            for odd, pick in ((0, lanes_lo), (1, lanes_hi)):
                if index is None:
                    ref[2 * t + odd] = pick(a, b)
                else:
                    ref[2 * t + odd, index] = pick(a, b)

    put(qk_ref, wq_ref, 0, True)
    put(qk_ref, wk_ref, 1, True)
    put(v_ref, wv_ref, None, False)


def row_proj(x, live, wq, wk, wv):
    w = pl.BlockSpec((E, 256), lambda n: (0, n))
    return pl.pallas_call(
        row_proj_kernel,
        grid=(3,),
        in_specs=[
            pl.BlockSpec((ROWS, E), lambda n: (0, 0)),
            pl.BlockSpec((ROWS, 1), lambda n: (0, 0)),
            w,
            w,
            w,
        ],
        out_specs=[
            pl.BlockSpec((4, 2, 256, 128), lambda n: (n, 0, 0, 0)),
            pl.BlockSpec((4, 256, 128), lambda n: (n, 0, 0)),
        ],
        out_shape=[
            jax.ShapeDtypeStruct((N, 2, 256, 128), bf16),
            jax.ShapeDtypeStruct((N, 256, 128), bf16),
        ],
        scratch_shapes=[pltpu.VMEM((ROWS, E), bf16)],
        compiler_params=params(),
        cost_estimate=cost(3 * 2 * ROWS * E * E, 8_000_000),
    )(x, live, wq, wk, wv)


def turn_kernel(x_ref, live_ref, wp_ref, xr_ref, wk_ref):
    r = lax.broadcasted_iota(jnp.int32, (ROWS, ROWS), 0)
    o = lax.broadcasted_iota(jnp.int32, (ROWS, ROWS), 1)
    src = ((r & 15) << 5) + ((r >> 5) << 1) + ((r >> 4) & 1)
    perm = jnp.where(src == o, 1.0, 0.0).astype(bf16)
    xr_ref[:, :E] = mm(perm, x_ref[...]).astype(bf16)
    mask = jnp.broadcast_to(live_ref[...], (ROWS, 128)).astype(bf16)
    xr_ref[:, E:] = mm(perm, mask).astype(bf16)
    wk_ref[...] = jnp.zeros_like(wk_ref)
    for c in range(C):
        w = wp_ref[C * c : C * c + C, :]
        for j in range(4):
            wk_ref[128 * c + 32 * j : 128 * c + 32 * j + 32, 128 * j : 128 * j + 128] = w


def turn(x, live, wp):
    return pl.pallas_call(
        turn_kernel,
        in_specs=whole(3),
        out_specs=whole(2),
        out_shape=[
            jax.ShapeDtypeStruct((ROWS, E + 128), bf16),
            jax.ShapeDtypeStruct((4096, 512), bf16),
        ],
        compiler_params=params(),
        cost_estimate=cost(2 * ROWS * ROWS * E, 8_000_000),
    )(x, live, wp)


def logits_kernel(qk_ref, out_ref):
    def side(k):
        return jnp.concatenate(
            [
                qk_ref[:, k, I * s : I * s + I, :].reshape(SITES, 128)
                for s in range(S // 2)
            ],
            axis=1,
        )

    out_ref[...] = mmt(side(0), side(1)) * (1.0 / math.sqrt(64 * SEQS))


def partial_logits(qk):
    return pl.pallas_call(
        logits_kernel,
        in_specs=whole(1),
        out_specs=pl.BlockSpec(memory_space=pltpu.VMEM),
        out_shape=jax.ShapeDtypeStruct((SITES, SITES), f32),
        compiler_params=params(),
        cost_estimate=cost(2 * SITES * SITES * 1024, 3_000_000),
    )(qk)


def softmax_kernel(in_ref, out_ref):
    total = in_ref[0]
    for k in range(1, N):
        total = total + in_ref[k]
    top = jnp.max(total, axis=-1, keepdims=True)
    e = jnp.exp(total - top)
    p = (e / jnp.sum(e, axis=-1, keepdims=True)).astype(bf16)
    for k in range(N):
        out_ref[k] = p


def row_softmax(parts):
    return pl.pallas_call(
        softmax_kernel,
        in_specs=whole(1),
        out_specs=pl.BlockSpec(memory_space=pltpu.VMEM),
        out_shape=jax.ShapeDtypeStruct((N, I, SITES), bf16),
        compiler_params=params(),
        cost_estimate=cost(N * I * SITES, 1_500_000, I * SITES),
    )(parts)


def row_mix_kernel(p_ref, v_ref, out_ref):
    v = jnp.concatenate(
        [v_ref[:, I * s : I * s + I, :].reshape(SITES, 128) for s in range(S // 2)],
        axis=1,
    )
    mix = mm(p_ref[...], v).astype(bf16)
    r = lax.broadcasted_iota(jnp.int32, (256, 256), 0)
    o = lax.broadcasted_iota(jnp.int32, (256, 256), 1)
    perm = jnp.where(((r & 7) << 5) + (r >> 3) == o, 1.0, 0.0).astype(bf16)

    def block(b):
        part = mix[I * b : I * b + I, :]
        return jnp.concatenate(
            [part[:, 128 * s : 128 * s + 128] for s in range(8)], axis=0
        )

    for b in range(0, N, 2):
        pair = jnp.concatenate([block(b), block(b + 1)], axis=1)
        turned = mm(perm, pair).astype(bf16)
        out_ref[256 * b : 256 * b + 256, :] = turned[:, :128]
        out_ref[256 * b + 256 : 256 * b + 512, :] = turned[:, 128:]


def row_mix(p, v):
    return pl.pallas_call(
        row_mix_kernel,
        in_specs=whole(2),
        out_specs=pl.BlockSpec(memory_space=pltpu.VMEM),
        out_shape=jax.ShapeDtypeStruct((4096, 128), bf16),
        compiler_params=params(),
        cost_estimate=cost(2 * SITES * SITES * 1024, 3_000_000),
    )(p, v)


def column_kernel(
    mr_ref, xc_ref, wo_ref, cq_ref, ck_ref, cv_ref, co_ref, f_ref,
    ao_ref, l_ref, r_ref,
    ysc, xsc, qs, ks, vs, ms,
):
    halves = []
    for pick in (lanes_lo, lanes_hi):
        halves.append(
            jnp.concatenate(
                [
                    pick(mr_ref[512 * t : 512 * t + 256, :], mr_ref[512 * t + 256 : 512 * t + 512, :])
                    for t in range(H // 2)
                ],
                axis=1,
            )
        )
    mixed = jnp.concatenate(halves, axis=0)
    ysc[...] = mm(mixed, wo_ref[...]).reshape(2, N, 2, 8, E)
    xsc[...] = xc_ref[...].astype(f32).reshape(N, 2, 2, 8, E + 128)
    blocks = []
    masks = []
    for i in range(2):
        for s2 in range(2):
            blocks.append((ysc[s2, :, i] + xsc[:, i, s2, :, :E]).reshape(128, E))
            masks.append(xsc[:, i, s2, :, E:].reshape(128, 128))
    after_rows = jnp.concatenate(blocks, axis=0).astype(bf16)
    wide = after_rows.astype(f32)
    mask = jnp.concatenate(masks, axis=0).astype(bf16)
    lane0 = jnp.where(
        lax.broadcasted_iota(jnp.int32, (8, 128), 1) == 0, 1.0, 0.0
    ).astype(bf16)
    alive = mmt(lane0, mask)

    normed = norm(wide)
    qs[...] = mm(normed, cq_ref[...]).astype(bf16)
    ks[...] = mm(normed, ck_ref[...]).astype(bf16)
    vs[...] = mm(normed, cv_ref[...]).astype(bf16)
    low = lax.broadcasted_iota(jnp.int32, (SEQS, 128), 1) < 64
    for i in range(2):
        rows = slice(SEQS * i, SEQS * i + SEQS)
        keep = alive[0:1, rows] > 0
        for t in range(H // 2):
            lanes = slice(128 * t, 128 * t + 128)
            q, k, v = qs[rows, lanes], ks[rows, lanes], vs[rows, lanes]
            mixes = []
            for own in (low, jnp.logical_not(low)):
                logits = mmt(jnp.where(own, q, jnp.zeros_like(q)), k) * 0.125
                logits = jnp.where(keep, logits, -1000000000.0)
                e = jnp.exp(logits - jnp.max(logits, axis=-1, keepdims=True))
                p = (e * (1.0 / jnp.sum(e, axis=-1, keepdims=True))).astype(bf16)
                mixes.append(mm(p, v))
            ms[rows, lanes] = jnp.where(low, mixes[0], mixes[1]).astype(bf16)

    out = (wide + mm(ms[...], co_ref[...])).astype(bf16)
    out_wide = out.astype(f32)
    for i in range(2):
        for s2 in range(2):
            at = SEQS * i + 128 * s2
            xsc[:, i, s2, :, :E] = out_wide[at : at + 128].reshape(N, 8, E)
    ao_ref[...] = xsc[:, :, :, :, :E].reshape(ROWS, E).astype(bf16)

    factors = (mmt(f_ref[...], norm(out_wide)) * alive[0:1, :]).astype(bf16)
    for ref, at in ((l_ref, 0), (r_ref, C)):
        for i in range(2):
            ref[C * i : C * i + C, :] = factors[at : at + C, SEQS * i : SEQS * i + SEQS]
        counts = [
            jnp.sum(alive[0:1, SEQS * i : SEQS * i + SEQS], axis=-1, keepdims=True)
            for i in range(2)
        ]
        row = lax.broadcasted_iota(jnp.int32, (LR - 2 * C, SEQS), 0)
        ref[2 * C :, :] = jnp.where(row == 0, counts[0], counts[1]).astype(bf16)


def column_step(mr, xc, wo, cq, ck, cv, co, f):
    return pl.pallas_call(
        column_kernel,
        in_specs=whole(8),
        out_specs=whole(3),
        out_shape=[
            jax.ShapeDtypeStruct((ROWS, E), bf16),
            jax.ShapeDtypeStruct((LR, SEQS), bf16),
            jax.ShapeDtypeStruct((LR, SEQS), bf16),
        ],
        scratch_shapes=[
            pltpu.VMEM((2, N, 2, 8, E), f32),
            pltpu.VMEM((N, 2, 2, 8, E + 128), f32),
            pltpu.VMEM((ROWS, E), bf16),
            pltpu.VMEM((ROWS, E), bf16),
            pltpu.VMEM((ROWS, E), bf16),
            pltpu.VMEM((ROWS, E), bf16),
        ],
        compiler_params=params(),
        cost_estimate=cost(5 * 2 * ROWS * E * E, 9_000_000, 2 * H * SEQS * SEQS),
    )(mr, xc, wo, cq, ck, cv, co, f)


def back_kernel(in_ref, out_ref):
    o = lax.broadcasted_iota(jnp.int32, (ROWS, ROWS), 0)
    r = lax.broadcasted_iota(jnp.int32, (ROWS, ROWS), 1)
    src = (((o >> 1) & 15) << 5) + ((o & 1) << 4) + (o >> 5)
    perm = jnp.where(src == r, 1.0, 0.0).astype(bf16)
    out_ref[...] = mm(perm, in_ref[...]).astype(bf16)


def back(rows):
    return pl.pallas_call(
        back_kernel,
        in_specs=whole(1),
        out_specs=pl.BlockSpec(memory_space=pltpu.VMEM),
        out_shape=jax.ShapeDtypeStruct((ROWS, E), bf16),
        compiler_params=params(),
        cost_estimate=cost(2 * ROWS * ROWS * E, 2_000_000),
    )(rows)


def pair_kernel(l_ref, r_ref, wk_ref, out_ref, lf, lg, lp, lhs, osc):
    every = l_ref[...].reshape(N * LR, SEQS).astype(f32)
    for k, ref in enumerate((lf, lg)):
        ref[...] = every[:, 128 * k : 128 * k + 128]

    def across(ref, start):
        return jnp.concatenate(
            [ref[pl.ds(start + i, N, stride=LR), :] for i in (0, C)], axis=0
        )

    for c in range(C):
        lp[C * c : C * c + C, :128] = across(lf, c).astype(bf16)
        lp[C * c : C * c + C, 128:] = across(lg, c).astype(bf16)
    left_count = jnp.concatenate(
        [lf[pl.ds(2 * C + i, N, stride=LR), :] for i in range(2)], axis=0
    )
    right = r_ref[:, : 2 * C, :].reshape(N * 2 * C, SEQS)
    for c in range(0, C, 4):
        outer = mmt(lp[C * c : C * c + 4 * C, :], right).astype(bf16)
        for k in range(4):
            for j in range(8):
                lhs[C * j : C * j + C, 128 * (c + k) : 128 * (c + k) + 128] = outer[
                    C * k : C * k + C, 128 * j : 128 * j + 128
                ]
    acc = mm(lhs[...], wk_ref[...])
    for j in range(C):
        part = acc[C * (j // 4) : C * (j // 4) + C, 128 * (j % 4) : 128 * (j % 4) + 128]
        right_count = r_ref[j >> 1, 2 * C : LR, :128].astype(f32)[(j & 1) : (j & 1) + 1, :]
        part = part / (jnp.minimum(left_count, right_count) + 0.001)
        for i in range(2):
            osc[pl.ds(C * i + j, N, stride=2 * C), :] = part[N * i : N * i + N, :]
    out_ref[...] = osc[...].astype(bf16)


def pair_step(left, right, wk):
    return pl.pallas_call(
        pair_kernel,
        in_specs=whole(3),
        out_specs=pl.BlockSpec(memory_space=pltpu.VMEM),
        out_shape=jax.ShapeDtypeStruct((C * C, PC), bf16),
        scratch_shapes=[
            pltpu.VMEM((N * LR, 128), f32),
            pltpu.VMEM((N * LR, 128), f32),
            pltpu.VMEM((1024, SEQS), bf16),
            pltpu.VMEM((256, 4096), bf16),
            pltpu.VMEM((1024, PC), f32),
        ],
        compiler_params=params(),
        cost_estimate=cost(2 * 1024 * 1024 * 256 + 2 * 256 * 4096 * 512, 6_000_000),
    )(left, right, wk)


def exchange(x, axis):
    return lax.all_to_all(x, axis, split_axis=0, concat_axis=0, tiled=True)


def on_device(x, occupancy, wq, wk, wv, wo, cq, ck, cv, co, f1, f2, wp):
    x = x.reshape(ROWS, E)
    live = occupancy.astype(f32).reshape(ROWS, 1)
    factors = jnp.concatenate([f1.T, f2.T], axis=0)

    qk, v = row_proj(x, live, wq, wk, wv)
    qk = exchange(qk.reshape(N, 512, 128), "cols").reshape(N, 2, 256, 128)
    xr, pair_w = turn(x, live, wp)
    xc = exchange(xr.reshape(N, 32, E + 128), "depth").reshape(ROWS, E + 128)
    v, qk = lax.optimization_barrier((v, qk))
    v = exchange(v, "cols")

    parts = exchange(partial_logits(qk).reshape(N, I, SITES), "depth")
    p = exchange(row_softmax(parts), "depth").reshape(SITES, SITES)
    mix = row_mix(p, v)
    mr = exchange(mix.reshape(N * N, 16, 128), ("cols", "depth")).reshape(4096, 128)

    rows, left, right = column_step(mr, xc, wo, cq, ck, cv, co, factors)
    right = lax.ppermute(
        right, ("depth", "cols"), [(N * d + g, N * g + d) for d in range(N) for g in range(N)]
    )
    left = exchange(jnp.broadcast_to(left[None], (N, LR, SEQS)), "depth")
    right = exchange(jnp.broadcast_to(right[None], (N, LR, SEQS)), "cols")
    rows = exchange(rows.reshape(N, 32, E), "depth")
    out = back(rows.reshape(ROWS, E)).reshape(S, I, E)
    pair = pair_step(left, right, pair_w).reshape(C, C, PC)
    return out, pair


def solution(mesh):
    placed = (P("depth", "cols", None), P("depth", "cols")) + (P(),) * 11
    return jax.shard_map(
        on_device,
        mesh=mesh,
        in_specs=placed,
        out_specs=(P("depth", "cols", None), P("cols", "depth", None)),
        check_vma=False,
    )
```

```python
import functools
import math

import jax
import jax.numpy as jnp
from jax import lax
from jax.experimental import pallas as pl
from jax.experimental.pallas import tpu as pltpu
from jax.sharding import PartitionSpec as P

f32 = jnp.float32
bf16 = jnp.bfloat16

S = 16
I = 32
E = 768
H = 12
N = 16
ROWS = S * I
SEQS = 256
SITES = 512
C = 32
PC = 128
XW = E + 128

NT = (((1,), (1,)), ((), ()))


def norm(wide):
    center = wide - jnp.mean(wide, axis=-1, keepdims=True)
    spread = jnp.mean(center * center, axis=-1, keepdims=True)
    return (center * lax.rsqrt(spread + 1e-05)).astype(bf16)


def mm(a, b):
    return jnp.dot(a, b, preferred_element_type=f32)


def mmt(a, b):
    return lax.dot_general(a, b, NT, preferred_element_type=f32)


def lanes_lo(a, b):
    return jnp.concatenate([a[:, :64], b[:, :64]], axis=1)


def lanes_hi(a, b):
    return jnp.concatenate([a[:, 64:], b[:, 64:]], axis=1)


def whole(n):
    return [pl.BlockSpec(memory_space=pltpu.VMEM)] * n


def params(mib):
    return pltpu.CompilerParams(vmem_limit_bytes=mib * 1024 * 1024)


def cost(flops, bytes_accessed, transcendentals=0):
    return pl.CostEstimate(
        flops=flops, bytes_accessed=bytes_accessed, transcendentals=transcendentals
    )


def mask_rows(occupancy, width):
    s = lax.broadcasted_iota(jnp.int32, (ROWS, S), 0) // I
    own = s == lax.broadcasted_iota(jnp.int32, (ROWS, S), 1)
    spread = mm(jnp.where(own, 1.0, 0.0).astype(bf16), occupancy.astype(f32).astype(bf16))
    i = lax.broadcasted_iota(jnp.int32, (ROWS, I), 0) % I
    own = i == lax.broadcasted_iota(jnp.int32, (ROWS, I), 1)
    column = jnp.sum(jnp.where(own, spread, 0.0), axis=-1, keepdims=True)
    return jnp.broadcast_to(column, (ROWS, width))


def row_proj_kernel(x_ref, occ_ref, wq_ref, wk_ref, wv_ref, out_ref, xn_ref, live_ref):
    @pl.when(pl.program_id(0) == 0)
    def _():
        xn_ref[...] = norm(x_ref[...].astype(f32))
        live_ref[...] = mask_rows(occ_ref[...], 128)

    xn = xn_ref[...]
    live = live_ref[...]
    half = ROWS // 2
    for index, w_ref in enumerate((wq_ref, wk_ref, wv_ref)):
        y = mm(xn, w_ref[...])
        for t in range(2):
            part = y[:, 128 * t : 128 * t + 128]
            if index < 2:
                part = part * live
            part = part.astype(bf16)
            a, b = part[:half], part[half:]
            out_ref[2 * t, 256 * index : 256 * index + 256] = lanes_lo(a, b)
            out_ref[2 * t + 1, 256 * index : 256 * index + 256] = lanes_hi(a, b)


def row_proj(x, occupancy, wq, wk, wv):
    w = pl.BlockSpec((E, 256), lambda n: (0, n))
    return pl.pallas_call(
        row_proj_kernel,
        grid=(3,),
        in_specs=[
            pl.BlockSpec((ROWS, E), lambda n: (0, 0)),
            pl.BlockSpec((S, I), lambda n: (0, 0)),
            w,
            w,
            w,
        ],
        out_specs=pl.BlockSpec((4, 768, 128), lambda n: (n, 0, 0)),
        out_shape=jax.ShapeDtypeStruct((N, 768, 128), bf16),
        scratch_shapes=[pltpu.VMEM((ROWS, E), bf16), pltpu.VMEM((ROWS, 128), f32)],
        compiler_params=params(20),
        cost_estimate=cost(3 * 2 * ROWS * E * E, 8_000_000),
    )(x, occupancy, wq, wk, wv)


def turn_kernel(x_ref, occ_ref, wp_ref, xr_ref, wk_ref):
    r = lax.broadcasted_iota(jnp.int32, (ROWS, ROWS), 0)
    o = lax.broadcasted_iota(jnp.int32, (ROWS, ROWS), 1)
    src = ((r & 15) << 5) + ((r >> 5) << 1) + ((r >> 4) & 1)
    perm = jnp.where(src == o, 1.0, 0.0).astype(bf16)
    xr_ref[:, :E] = mm(perm, x_ref[...]).astype(bf16)
    xr_ref[:, E:] = mm(perm, mask_rows(occ_ref[...], 128).astype(bf16)).astype(bf16)
    wk_ref[...] = jnp.zeros_like(wk_ref)
    for c in range(C):
        w = wp_ref[C * c : C * c + C, :]
        for j in range(4):
            wk_ref[128 * c + 32 * j : 128 * c + 32 * j + 32, 128 * j : 128 * j + 128] = w


def turn(x, occupancy, wp):
    return pl.pallas_call(
        turn_kernel,
        in_specs=whole(3),
        out_specs=whole(2),
        out_shape=[
            jax.ShapeDtypeStruct((ROWS, XW), bf16),
            jax.ShapeDtypeStruct((4096, 512), bf16),
        ],
        compiler_params=params(16),
        cost_estimate=cost(2 * ROWS * ROWS * E, 8_000_000),
    )(x, occupancy, wp)


def logits_kernel(qk_ref, out_ref):
    def side(k):
        return jnp.concatenate(
            [
                qk_ref[:, 256 * k + I * s : 256 * k + I * s + I, :].reshape(SITES, 128)
                for s in range(S // 2)
            ],
            axis=1,
        )

    out_ref[...] = mmt(side(0), side(1)) * (1.0 / math.sqrt(64 * SEQS))


def partial_logits(qkv):
    return pl.pallas_call(
        logits_kernel,
        grid=(1,),
        in_specs=[pl.BlockSpec((N, 512, 128), lambda n: (0, 0, 0))],
        out_specs=pl.BlockSpec((SITES, SITES), lambda n: (0, 0)),
        out_shape=jax.ShapeDtypeStruct((SITES, SITES), f32),
        compiler_params=params(20),
        cost_estimate=cost(2 * SITES * SITES * 1024, 3_000_000),
    )(qkv)


def softmax_kernel(in_ref, xr_ref, out_ref):
    total = in_ref[0]
    for k in range(1, N):
        total = total + in_ref[k]
    top = jnp.max(total, axis=-1, keepdims=True)
    e = jnp.exp(total - top)
    p = (e / jnp.sum(e, axis=-1, keepdims=True)).astype(bf16)
    for k in range(N):
        out_ref[k, :, :SITES] = p
    out_ref[:, :, SITES:] = xr_ref[...].reshape(N, I, XW)


def row_softmax(parts, xr):
    return pl.pallas_call(
        softmax_kernel,
        in_specs=whole(2),
        out_specs=pl.BlockSpec(memory_space=pltpu.VMEM),
        out_shape=jax.ShapeDtypeStruct((N, I, SITES + XW), bf16),
        compiler_params=params(16),
        cost_estimate=cost(N * I * SITES, 4_000_000, I * SITES),
    )(parts, xr)


def row_mix_kernel(p_ref, v_ref, out_ref):
    v = jnp.concatenate(
        [v_ref[:, I * s : I * s + I, :].reshape(SITES, 128) for s in range(S // 2)],
        axis=1,
    )
    mix = mm(p_ref[...].reshape(SITES, SITES), v).astype(bf16)
    r = lax.broadcasted_iota(jnp.int32, (256, 256), 0)
    o = lax.broadcasted_iota(jnp.int32, (256, 256), 1)
    perm = jnp.where(((r & 7) << 5) + (r >> 3) == o, 1.0, 0.0).astype(bf16)

    def block(b):
        part = mix[I * b : I * b + I, :]
        return jnp.concatenate(
            [part[:, 128 * s : 128 * s + 128] for s in range(8)], axis=0
        )

    for b in range(0, N, 2):
        pair = jnp.concatenate([block(b), block(b + 1)], axis=1)
        turned = mm(perm, pair).astype(bf16)
        out_ref[256 * b : 256 * b + 256, :] = turned[:, :128]
        out_ref[256 * b + 256 : 256 * b + 512, :] = turned[:, 128:]


def row_mix(px, qkv):
    return pl.pallas_call(
        row_mix_kernel,
        grid=(1,),
        in_specs=[
            pl.BlockSpec((N, I, SITES), lambda n: (0, 0, 0)),
            pl.BlockSpec((N, 256, 128), lambda n: (0, 2, 0)),
        ],
        out_specs=pl.BlockSpec((4096, 128), lambda n: (0, 0)),
        out_shape=jax.ShapeDtypeStruct((4096, 128), bf16),
        compiler_params=params(20),
        cost_estimate=cost(2 * SITES * SITES * 1024, 3_000_000),
    )(px, qkv)


def column_kernel(
    mr_ref, px_ref, wo_ref, cq_ref, ck_ref, cv_ref, co_ref, f_ref,
    out_ref, r_ref,
    ysc, xsc, qs, ks, vs, ms,
):
    halves = []
    for pick in (lanes_lo, lanes_hi):
        halves.append(
            jnp.concatenate(
                [
                    pick(mr_ref[512 * t : 512 * t + 256, :], mr_ref[512 * t + 256 : 512 * t + 512, :])
                    for t in range(H // 2)
                ],
                axis=1,
            )
        )
    mixed = jnp.concatenate(halves, axis=0)
    ysc[...] = mm(mixed, wo_ref[...]).reshape(2, N, 2, 8, E)
    xsc[...] = px_ref[:, :, SITES:].astype(f32).reshape(N, 2, 2, 8, XW)
    blocks = []
    masks = []
    for i in range(2):
        for s2 in range(2):
            blocks.append((ysc[s2, :, i] + xsc[:, i, s2, :, :E]).reshape(128, E))
            masks.append(xsc[:, i, s2, :, E:].reshape(128, 128))
    after_rows = jnp.concatenate(blocks, axis=0).astype(bf16)
    wide = after_rows.astype(f32)
    mask = jnp.concatenate(masks, axis=0).astype(bf16)
    lane0 = jnp.where(
        lax.broadcasted_iota(jnp.int32, (8, 128), 1) == 0, 1.0, 0.0
    ).astype(bf16)
    alive = mmt(lane0, mask)

    normed = norm(wide)
    qs[...] = mm(normed, cq_ref[...]).astype(bf16)
    ks[...] = mm(normed, ck_ref[...]).astype(bf16)
    vs[...] = mm(normed, cv_ref[...]).astype(bf16)
    low = lax.broadcasted_iota(jnp.int32, (SEQS, 128), 1) < 64
    for i in range(2):
        rows = slice(SEQS * i, SEQS * i + SEQS)
        keep = alive[0:1, rows] > 0
        for t in range(H // 2):
            lanes = slice(128 * t, 128 * t + 128)
            q, k, v = qs[rows, lanes], ks[rows, lanes], vs[rows, lanes]
            mixes = []
            for own in (low, jnp.logical_not(low)):
                logits = mmt(jnp.where(own, q, jnp.zeros_like(q)), k) * 0.125
                logits = jnp.where(keep, logits, -1000000000.0)
                e = jnp.exp(logits - jnp.max(logits, axis=-1, keepdims=True))
                p = (e * (1.0 / jnp.sum(e, axis=-1, keepdims=True))).astype(bf16)
                mixes.append(mm(p, v))
            ms[rows, lanes] = jnp.where(low, mixes[0], mixes[1]).astype(bf16)

    out = (wide + mm(ms[...], co_ref[...])).astype(bf16)
    out_wide = out.astype(f32)
    for i in range(2):
        for s2 in range(2):
            at = SEQS * i + 128 * s2
            xsc[:, i, s2, :, :E] = out_wide[at : at + 128].reshape(N, 8, E)
    out_ref[:, :I, :] = xsc[:, :, :, :, :E].reshape(N, I, E).astype(bf16)

    factors = (mmt(f_ref[...], norm(out_wide)) * alive[0:1, :]).astype(bf16)
    for i in range(2):
        r_ref[C * i : C * i + C, :] = factors[C:, SEQS * i : SEQS * i + SEQS]
    counts = [
        jnp.sum(alive[0:1, SEQS * i : SEQS * i + SEQS], axis=-1, keepdims=True)
        for i in range(2)
    ]
    row = lax.broadcasted_iota(jnp.int32, (C, SEQS), 0)
    count = jnp.where(row == 0, counts[0], counts[1]).astype(bf16)
    left = jnp.concatenate([factors[:C, :], count], axis=1)
    for k in range(N):
        out_ref[k, I:, :] = left


def column_step(mr, px, wo, cq, ck, cv, co, f):
    return pl.pallas_call(
        column_kernel,
        in_specs=whole(8),
        out_specs=whole(2),
        out_shape=[
            jax.ShapeDtypeStruct((N, 2 * I, E), bf16),
            jax.ShapeDtypeStruct((2 * C, SEQS), bf16),
        ],
        scratch_shapes=[
            pltpu.VMEM((2, N, 2, 8, E), f32),
            pltpu.VMEM((N, 2, 2, 8, XW), f32),
            pltpu.VMEM((ROWS, E), bf16),
            pltpu.VMEM((ROWS, E), bf16),
            pltpu.VMEM((ROWS, E), bf16),
            pltpu.VMEM((ROWS, E), bf16),
        ],
        compiler_params=params(40),
        cost_estimate=cost(5 * 2 * ROWS * E * E, 9_000_000, 2 * H * SEQS * SEQS),
    )(mr, px, wo, cq, ck, cv, co, f)


def back_kernel(in_ref, out_ref):
    o = lax.broadcasted_iota(jnp.int32, (ROWS, ROWS), 0)
    r = lax.broadcasted_iota(jnp.int32, (ROWS, ROWS), 1)
    src = (((o >> 1) & 15) << 5) + ((o & 1) << 4) + (o >> 5)
    perm = jnp.where(src == r, 1.0, 0.0).astype(bf16)
    out_ref[...] = mm(perm, in_ref[...].reshape(ROWS, E)).astype(bf16)


def back(both):
    return pl.pallas_call(
        back_kernel,
        grid=(1,),
        in_specs=[pl.BlockSpec((N, I, E), lambda n: (0, 0, 0))],
        out_specs=pl.BlockSpec((ROWS, E), lambda n: (0, 0)),
        out_shape=jax.ShapeDtypeStruct((ROWS, E), bf16),
        compiler_params=params(16),
        cost_estimate=cost(2 * ROWS * ROWS * E, 2_000_000),
    )(both)


def pair_kernel(l_ref, r_ref, n_ref, wk_ref, out_ref, l0, l1, l2, l3, l4, lp, lhs, osc):
    every = l_ref[...].reshape(N * C, E).astype(f32)
    for k, ref in enumerate((l0, l1, l2, l3, l4)):
        ref[...] = every[:, 128 * k : 128 * k + 128]

    def across(ref, row):
        return ref[pl.ds(row, N, stride=C), :]

    for c in range(C):
        rows = slice(C * c, C * c + C)
        lp[rows, :128] = jnp.concatenate([across(l0, c), across(l2, c)], axis=0).astype(bf16)
        lp[rows, 128:] = jnp.concatenate([across(l1, c), across(l3, c)], axis=0).astype(bf16)
    left_count = jnp.concatenate([across(l4, 0), across(l4, 1)], axis=0)
    right = r_ref[...].reshape(N * 2 * C, SEQS)
    for c in range(0, C, 4):
        outer = mmt(lp[C * c : C * c + 4 * C, :], right).astype(bf16)
        for k in range(4):
            for j in range(8):
                lhs[C * j : C * j + C, 128 * (c + k) : 128 * (c + k) + 128] = outer[
                    C * k : C * k + C, 128 * j : 128 * j + 128
                ]
    acc = mm(lhs[...], wk_ref[...])
    right_count = n_ref[...].astype(f32)
    for j in range(C):
        part = acc[C * (j // 4) : C * (j // 4) + C, 128 * (j % 4) : 128 * (j % 4) + 128]
        part = part / (jnp.minimum(left_count, right_count[j : j + 1, :]) + 0.001)
        for i in range(2):
            osc[pl.ds(C * i + j, N, stride=2 * C), :] = part[N * i : N * i + N, :]
    out_ref[...] = osc[...].astype(bf16)


def pair_step(both, right, counts, wk):
    return pl.pallas_call(
        pair_kernel,
        grid=(1,),
        in_specs=[
            pl.BlockSpec((N, I, E), lambda n: (0, 1, 0)),
            pl.BlockSpec((N, 2 * C, SEQS), lambda n: (0, 0, 0)),
            pl.BlockSpec((C, 128), lambda n: (0, 0)),
            pl.BlockSpec((4096, 512), lambda n: (0, 0)),
        ],
        out_specs=pl.BlockSpec((C * C, PC), lambda n: (0, 0)),
        out_shape=jax.ShapeDtypeStruct((C * C, PC), bf16),
        scratch_shapes=[pltpu.VMEM((N * C, 128), f32)] * 5
        + [
            pltpu.VMEM((1024, SEQS), bf16),
            pltpu.VMEM((256, 4096), bf16),
            pltpu.VMEM((1024, PC), f32),
        ],
        compiler_params=params(24),
        cost_estimate=cost(2 * 1024 * 1024 * 256 + 2 * 256 * 4096 * 512, 6_000_000),
    )(both, right, counts, wk)


def exchange(x, axis):
    return lax.all_to_all(x, axis, split_axis=0, concat_axis=0, tiled=True)


def swap(x):
    pairs = [(N * d + g, N * g + d) for d in range(N) for g in range(N)]
    return lax.ppermute(x, ("depth", "cols"), pairs)


def on_device(x, occupancy, wq, wk, wv, wo, cq, ck, cv, co, f1, f2, wp):
    x = x.reshape(ROWS, E)
    factors = jnp.concatenate([f1.T, f2.T], axis=0)

    qkv = exchange(row_proj(x, occupancy, wq, wk, wv), "cols")
    xr, pair_w = turn(x, occupancy, wp)
    parts = exchange(partial_logits(qkv).reshape(N, I, SITES), "depth")
    px = exchange(row_softmax(parts, xr), "depth")
    mix = row_mix(px, qkv)
    mr = exchange(mix.reshape(N * N, 16, 128), ("cols", "depth")).reshape(4096, 128)

    both, right = column_step(mr, px, wo, cq, ck, cv, co, factors)
    right = swap(right)
    both = exchange(both, "depth")
    counts = swap(both[:, I : I + 2, 512:640].reshape(C, 128))
    right = exchange(jnp.broadcast_to(right[None], (N, 2 * C, SEQS)), "cols")
    out = back(both).reshape(S, I, E)
    pair = pair_step(both, right, counts, pair_w).reshape(C, C, PC)
    return out, pair


def solution(mesh):
    placed = (P("depth", "cols", None), P("depth", "cols")) + (P(),) * 11
    return jax.shard_map(
        on_device,
        mesh=mesh,
        in_specs=placed,
        out_specs=(P("depth", "cols", None), P("cols", "depth", None)),
        check_vma=False,
    )
```

```python
import functools
import math

import jax
import jax.numpy as jnp
from jax import lax
from jax.experimental import pallas as pl
from jax.experimental.pallas import tpu as pltpu
from jax.sharding import PartitionSpec as P

f32 = jnp.float32
bf16 = jnp.bfloat16

S = 16
I = 32
E = 768
H = 12
N = 16
ROWS = S * I
SEQS = 256
SITES = 512
C = 32
PC = 128
XW = E + 128

NT = (((1,), (1,)), ((), ()))


def norm(wide):
    center = wide - jnp.mean(wide, axis=-1, keepdims=True)
    spread = jnp.mean(center * center, axis=-1, keepdims=True)
    return (center * lax.rsqrt(spread + 1e-05)).astype(bf16)


def mm(a, b):
    return jnp.dot(a, b, preferred_element_type=f32)


def mmt(a, b):
    return lax.dot_general(a, b, NT, preferred_element_type=f32)


def lanes_lo(a, b):
    return jnp.concatenate([a[:, :64], b[:, :64]], axis=1)


def lanes_hi(a, b):
    return jnp.concatenate([a[:, 64:], b[:, 64:]], axis=1)


HBM = pl.BlockSpec(memory_space=pltpu.HBM)


def whole(n):
    return [pl.BlockSpec(memory_space=pltpu.VMEM)] * n


def params(mib):
    return pltpu.CompilerParams(vmem_limit_bytes=int(mib * 1024 * 1024))


def cost(flops, bytes_accessed, transcendentals=0):
    return pl.CostEstimate(
        flops=flops, bytes_accessed=bytes_accessed, transcendentals=transcendentals
    )


def mask_rows(occupancy, width):
    s = lax.broadcasted_iota(jnp.int32, (ROWS, S), 0) // I
    own = s == lax.broadcasted_iota(jnp.int32, (ROWS, S), 1)
    spread = mm(jnp.where(own, 1.0, 0.0).astype(bf16), occupancy.astype(f32).astype(bf16))
    i = lax.broadcasted_iota(jnp.int32, (ROWS, I), 0) % I
    own = i == lax.broadcasted_iota(jnp.int32, (ROWS, I), 1)
    column = jnp.sum(jnp.where(own, spread, 0.0), axis=-1, keepdims=True)
    return jnp.broadcast_to(column, (ROWS, width))


def row_proj_kernel(
    x_hbm, occ_hbm, wq_hbm, wk_hbm, wv_hbm, out_hbm, xr_hbm,
    xv, occ, wv, xn_ref, out, xr, sems,
):
    first = [pltpu.make_async_copy(occ_hbm, occ, sems.at[0])]
    for k in range(4):
        rows = pl.ds(128 * k, 128)
        first.append(pltpu.make_async_copy(x_hbm.at[rows], xv.at[rows], sems.at[1 + k]))
    for copy in first:
        copy.start()
    tiles = [
        pltpu.make_async_copy(w, wv.at[k], sems.at[5 + k])
        for k, w in enumerate((wq_hbm, wk_hbm, wv_hbm))
    ]
    first[0].wait()
    live = mask_rows(occ[...], 128)
    for k in range(4):
        first[1 + k].wait()
        if k == 0:
            tiles[0].start()
        rows = slice(128 * k, 128 * k + 128)
        xn_ref[rows] = norm(xv[rows].astype(f32))
    for copy in tiles[1:]:
        copy.start()
    r = lax.broadcasted_iota(jnp.int32, (ROWS, ROWS), 0)
    o = lax.broadcasted_iota(jnp.int32, (ROWS, ROWS), 1)
    src = ((r & 15) << 5) + ((r >> 5) << 1) + ((r >> 4) & 1)
    perm = jnp.where(src == o, 1.0, 0.0).astype(bf16)
    xr[:, :E] = mm(perm, xv[...]).astype(bf16)
    xr[:, E:] = mm(perm, live.astype(bf16)).astype(bf16)
    sent = [pltpu.make_async_copy(xr, xr_hbm, sems.at[8])]
    sent[0].start()
    xn = xn_ref[...]
    half = ROWS // 2
    for index in range(3):
        tiles[index].wait()
        rows = slice(256 * index, 256 * index + 256)
        for n in range(3):
            y = mm(xn, wv[index, :, 256 * n : 256 * n + 256])
            for t in range(2):
                part = y[:, 128 * t : 128 * t + 128]
                if index < 2:
                    part = part * live
                part = part.astype(bf16)
                a, b = part[:half], part[half:]
                out[4 * n + 2 * t, rows] = lanes_lo(a, b)
                out[4 * n + 2 * t + 1, rows] = lanes_hi(a, b)
        at = pl.ds(256 * index, 256)
        sent.append(
            pltpu.make_async_copy(
                out.at[:, at], out_hbm.at[pl.ds(0, H), at], sems.at[9 + index]
            )
        )
        sent[-1].start()
    for copy in sent:
        copy.wait()


def row_proj(x, occupancy, wq, wk, wv):
    return pl.pallas_call(
        row_proj_kernel,
        in_specs=[HBM] * 5,
        out_specs=[HBM] * 2,
        out_shape=[
            jax.ShapeDtypeStruct((N, 768, 128), bf16),
            jax.ShapeDtypeStruct((ROWS, XW), bf16),
        ],
        scratch_shapes=[
            pltpu.VMEM((ROWS, E), bf16),
            pltpu.VMEM((S, I), jnp.int32),
            pltpu.VMEM((3, E, E), bf16),
            pltpu.VMEM((ROWS, E), bf16),
            pltpu.VMEM((H, 768, 128), bf16),
            pltpu.VMEM((ROWS, XW), bf16),
            pltpu.SemaphoreType.DMA((12,)),
        ],
        compiler_params=params(61),
        cost_estimate=cost(3 * 2 * ROWS * E * E, 8_000_000),
    )(x, occupancy, wq, wk, wv)


def logits_kernel(qk_ref, out_ref):
    def side(k):
        return jnp.concatenate(
            [
                qk_ref[:, 256 * k + I * s : 256 * k + I * s + I, :].reshape(SITES, 128)
                for s in range(S // 2)
            ],
            axis=1,
        )

    out_ref[...] = mmt(side(0), side(1)) * (1.0 / math.sqrt(64 * SEQS))


def partial_logits(qkv):
    return pl.pallas_call(
        logits_kernel,
        grid=(1,),
        in_specs=[pl.BlockSpec((N, 512, 128), lambda n: (0, 0, 0))],
        out_specs=pl.BlockSpec((SITES, SITES), lambda n: (0, 0)),
        out_shape=jax.ShapeDtypeStruct((SITES, SITES), f32),
        compiler_params=params(20),
        cost_estimate=cost(2 * SITES * SITES * 1024, 3_000_000),
    )(qkv)


def softmax_kernel(in_ref, xr_hbm, out_ref, sem):
    copy = pltpu.make_async_copy(xr_hbm, out_ref.at[:, :, pl.ds(SITES, XW)], sem)
    copy.start()
    total = in_ref[0]
    for k in range(1, N):
        total = total + in_ref[k]
    top = jnp.max(total, axis=-1, keepdims=True)
    e = jnp.exp(total - top)
    p = (e / jnp.sum(e, axis=-1, keepdims=True)).astype(bf16)
    for k in range(N):
        out_ref[k, :, :SITES] = p
    copy.wait()


def row_softmax(parts, xr):
    return pl.pallas_call(
        softmax_kernel,
        in_specs=whole(1) + [HBM],
        out_specs=pl.BlockSpec(memory_space=pltpu.VMEM),
        out_shape=jax.ShapeDtypeStruct((N, I, SITES + XW), bf16),
        scratch_shapes=[pltpu.SemaphoreType.DMA],
        compiler_params=params(16),
        cost_estimate=cost(N * I * SITES, 4_000_000, I * SITES),
    )(parts, xr)


def row_mix_kernel(p_ref, v_ref, out_ref):
    v = jnp.concatenate(
        [v_ref[:, I * s : I * s + I, :].reshape(SITES, 128) for s in range(S // 2)],
        axis=1,
    )
    mix = mm(p_ref[...].reshape(SITES, SITES), v).astype(bf16)
    r = lax.broadcasted_iota(jnp.int32, (256, 256), 0)
    o = lax.broadcasted_iota(jnp.int32, (256, 256), 1)
    perm = jnp.where(((r & 7) << 5) + (r >> 3) == o, 1.0, 0.0).astype(bf16)

    def block(b):
        part = mix[I * b : I * b + I, :]
        return jnp.concatenate(
            [part[:, 128 * s : 128 * s + 128] for s in range(8)], axis=0
        )

    for b in range(0, N, 2):
        pair = jnp.concatenate([block(b), block(b + 1)], axis=1)
        turned = mm(perm, pair).astype(bf16)
        out_ref[256 * b : 256 * b + 256, :] = turned[:, :128]
        out_ref[256 * b + 256 : 256 * b + 512, :] = turned[:, 128:]


def row_mix(px, qkv):
    return pl.pallas_call(
        row_mix_kernel,
        grid=(1,),
        in_specs=[
            pl.BlockSpec((N, I, SITES), lambda n: (0, 0, 0)),
            pl.BlockSpec((N, 256, 128), lambda n: (0, 2, 0)),
        ],
        out_specs=pl.BlockSpec((4096, 128), lambda n: (0, 0)),
        out_shape=jax.ShapeDtypeStruct((4096, 128), bf16),
        compiler_params=params(20),
        cost_estimate=cost(2 * SITES * SITES * 1024, 3_000_000),
    )(px, qkv)


def column_kernel(
    mr_ref, px_hbm, f1_ref, f2_ref, wo_hbm, cq_hbm, ck_hbm, cv_hbm, co_hbm,
    out_hbm, r_ref,
    ysc, xsc, qs, ks, vs, ms, weights, xb, ao, left, sems, out_sems,
):
    copies = []
    for k, w in enumerate((wo_hbm, cq_hbm, ck_hbm, cv_hbm, co_hbm)):
        copies.append(pltpu.make_async_copy(w, weights.at[k], sems.at[k]))
    fetch = pltpu.make_async_copy(px_hbm.at[:, :, pl.ds(SITES, XW)], xb, sems.at[5])
    copies[0].start()
    fetch.start()

    def weight(k):
        copies[k].wait()
        for more in ((1, 2), (3,), (4,), (), ())[k]:
            copies[more].start()
        return weights[k]

    halves = []
    for pick in (lanes_lo, lanes_hi):
        halves.append(
            jnp.concatenate(
                [
                    pick(mr_ref[512 * t : 512 * t + 256, :], mr_ref[512 * t + 256 : 512 * t + 512, :])
                    for t in range(H // 2)
                ],
                axis=1,
            )
        )
    mixed = jnp.concatenate(halves, axis=0)
    ysc[...] = mm(mixed, weight(0)).reshape(2, N, 2, 8, E)
    fetch.wait()
    xsc[...] = xb[...].astype(f32).reshape(N, 2, 2, 8, XW)
    blocks = []
    masks = []
    for i in range(2):
        for s2 in range(2):
            blocks.append((ysc[s2, :, i] + xsc[:, i, s2, :, :E]).reshape(128, E))
            masks.append(xsc[:, i, s2, :, E:].reshape(128, 128))
    after_rows = jnp.concatenate(blocks, axis=0).astype(bf16)
    wide = after_rows.astype(f32)
    mask = jnp.concatenate(masks, axis=0).astype(bf16)
    lane0 = jnp.where(
        lax.broadcasted_iota(jnp.int32, (8, 128), 1) == 0, 1.0, 0.0
    ).astype(bf16)
    alive = mmt(lane0, mask)

    normed = norm(wide)
    qs[...] = mm(normed, weight(1)).astype(bf16)
    ks[...] = mm(normed, weight(2)).astype(bf16)
    vs[...] = mm(normed, weight(3)).astype(bf16)
    low = lax.broadcasted_iota(jnp.int32, (SEQS, 128), 1) < 64
    for i in range(2):
        rows = slice(SEQS * i, SEQS * i + SEQS)
        keep = alive[0:1, rows] > 0
        for t in range(H // 2):
            lanes = slice(128 * t, 128 * t + 128)
            q, k, v = qs[rows, lanes], ks[rows, lanes], vs[rows, lanes]
            mixes = []
            for own in (low, jnp.logical_not(low)):
                logits = mmt(jnp.where(own, q, jnp.zeros_like(q)), k) * 0.125
                logits = jnp.where(keep, logits, -1000000000.0)
                e = jnp.exp(logits - jnp.max(logits, axis=-1, keepdims=True))
                p = (e * (1.0 / jnp.sum(e, axis=-1, keepdims=True))).astype(bf16)
                mixes.append(mm(p, v))
            ms[rows, lanes] = jnp.where(low, mixes[0], mixes[1]).astype(bf16)

    out = (wide + mm(ms[...], weight(4))).astype(bf16)
    out_wide = out.astype(f32)
    for i in range(2):
        for s2 in range(2):
            at = SEQS * i + 128 * s2
            xsc[:, i, s2, :, :E] = out_wide[at : at + 128].reshape(N, 8, E)
    ao[...] = xsc[:, :, :, :, :E].reshape(N, I, E).astype(bf16)
    sent = [pltpu.make_async_copy(ao, out_hbm.at[:, pl.ds(0, I)], out_sems.at[N])]
    sent[0].start()

    f = jnp.concatenate([f1_ref[...], f2_ref[...]], axis=0)
    factors = (mmt(f, norm(out_wide)) * alive[0:1, :]).astype(bf16)
    for i in range(2):
        r_ref[C * i : C * i + C, :] = factors[C:, SEQS * i : SEQS * i + SEQS]
    counts = [
        jnp.sum(alive[0:1, SEQS * i : SEQS * i + SEQS], axis=-1, keepdims=True)
        for i in range(2)
    ]
    row = lax.broadcasted_iota(jnp.int32, (C, SEQS), 0)
    count = jnp.where(row == 0, counts[0], counts[1]).astype(bf16)
    left[...] = jnp.concatenate([factors[:C, :], count], axis=1)
    for k in range(N):
        sent.append(pltpu.make_async_copy(left, out_hbm.at[k, pl.ds(I, C)], out_sems.at[k]))
        sent[-1].start()
    for copy in sent:
        copy.wait()


def column_step(mr, px, f1, f2, wo, cq, ck, cv, co):
    return pl.pallas_call(
        column_kernel,
        in_specs=whole(1) + [HBM] + whole(2) + [HBM] * 5,
        out_specs=[HBM, pl.BlockSpec(memory_space=pltpu.VMEM)],
        out_shape=[
            jax.ShapeDtypeStruct((N, 2 * I, E), bf16),
            jax.ShapeDtypeStruct((2 * C, SEQS), bf16),
        ],
        scratch_shapes=[
            pltpu.VMEM((2, N, 2, 8, E), f32),
            pltpu.VMEM((N, 2, 2, 8, XW), f32),
            pltpu.VMEM((ROWS, E), bf16),
            pltpu.VMEM((ROWS, E), bf16),
            pltpu.VMEM((ROWS, E), bf16),
            pltpu.VMEM((ROWS, E), bf16),
            pltpu.VMEM((5, E, E), bf16),
            pltpu.VMEM((N, I, XW), bf16),
            pltpu.VMEM((N, I, E), bf16),
            pltpu.VMEM((C, E), bf16),
            pltpu.SemaphoreType.DMA((6,)),
            pltpu.SemaphoreType.DMA((N + 1,)),
        ],
        compiler_params=params(59),
        cost_estimate=cost(5 * 2 * ROWS * E * E, 9_000_000, 2 * H * SEQS * SEQS),
    )(mr, px, f1, f2, wo, cq, ck, cv, co)


def back_kernel(in_ref, out_ref):
    o = lax.broadcasted_iota(jnp.int32, (ROWS, ROWS), 0)
    r = lax.broadcasted_iota(jnp.int32, (ROWS, ROWS), 1)
    src = (((o >> 1) & 15) << 5) + ((o & 1) << 4) + (o >> 5)
    perm = jnp.where(src == r, 1.0, 0.0).astype(bf16)
    out_ref[...] = mm(perm, in_ref[...].reshape(ROWS, E)).astype(bf16)


def back(both):
    return pl.pallas_call(
        back_kernel,
        grid=(1,),
        in_specs=[pl.BlockSpec((N, I, E), lambda n: (0, 0, 0))],
        out_specs=pl.BlockSpec((ROWS, E), lambda n: (0, 0)),
        out_shape=jax.ShapeDtypeStruct((ROWS, E), bf16),
        compiler_params=params(24),
        cost_estimate=cost(2 * ROWS * ROWS * E, 2_000_000),
    )(both)


def pair_kernel(
    l_ref, r_ref, n_ref, wp_ref, out_ref, l0, l1, l2, l3, l4, lp, lhs, osc, wk
):
    wk[...] = jnp.zeros_like(wk)
    for c in range(C):
        w = wp_ref[C * c : C * c + C, :]
        for j in range(4):
            at = 128 * c + C * j
            wk[at : at + C, 128 * j : 128 * j + 128] = w
    every = l_ref[...].reshape(N * C, E).astype(f32)
    for k, ref in enumerate((l0, l1, l2, l3, l4)):
        ref[...] = every[:, 128 * k : 128 * k + 128]

    def across(ref, row):
        return ref[pl.ds(row, N, stride=C), :]

    for c in range(C):
        rows = slice(C * c, C * c + C)
        lp[rows, :128] = jnp.concatenate([across(l0, c), across(l2, c)], axis=0).astype(bf16)
        lp[rows, 128:] = jnp.concatenate([across(l1, c), across(l3, c)], axis=0).astype(bf16)
    left_count = jnp.concatenate([across(l4, 0), across(l4, 1)], axis=0)
    right = r_ref[...].reshape(N * 2 * C, SEQS)
    for c in range(0, C, 4):
        outer = mmt(lp[C * c : C * c + 4 * C, :], right).astype(bf16)
        for k in range(4):
            for j in range(8):
                lhs[C * j : C * j + C, 128 * (c + k) : 128 * (c + k) + 128] = outer[
                    C * k : C * k + C, 128 * j : 128 * j + 128
                ]
    acc = mm(lhs[...], wk[...])
    right_count = n_ref[...].astype(f32)
    for j in range(C):
        part = acc[C * (j // 4) : C * (j // 4) + C, 128 * (j % 4) : 128 * (j % 4) + 128]
        part = part / (jnp.minimum(left_count, right_count[j : j + 1, :]) + 0.001)
        for i in range(2):
            osc[pl.ds(C * i + j, N, stride=2 * C), :] = part[N * i : N * i + N, :]
    out_ref[...] = osc[...].astype(bf16)


def pair_step(both, right, counts, wp):
    return pl.pallas_call(
        pair_kernel,
        grid=(1,),
        in_specs=[
            pl.BlockSpec((N, I, E), lambda n: (0, 1, 0)),
            pl.BlockSpec((N, 2 * C, SEQS), lambda n: (0, 0, 0)),
            pl.BlockSpec((C, 128), lambda n: (0, 0)),
            pl.BlockSpec((C * C, PC), lambda n: (0, 0)),
        ],
        out_specs=pl.BlockSpec((C * C, PC), lambda n: (0, 0)),
        out_shape=jax.ShapeDtypeStruct((C * C, PC), bf16),
        scratch_shapes=[pltpu.VMEM((N * C, 128), f32)] * 5
        + [
            pltpu.VMEM((1024, SEQS), bf16),
            pltpu.VMEM((256, 4096), bf16),
            pltpu.VMEM((1024, PC), f32),
            pltpu.VMEM((4096, 512), bf16),
        ],
        compiler_params=params(24),
        cost_estimate=cost(2 * 1024 * 1024 * 256 + 2 * 256 * 4096 * 512, 6_000_000),
    )(both, right, counts, wp)


def exchange(x, axis):
    return lax.all_to_all(x, axis, split_axis=0, concat_axis=0, tiled=True)


def swap(x):
    pairs = [(N * d + g, N * g + d) for d in range(N) for g in range(N)]
    return lax.ppermute(x, ("depth", "cols"), pairs)


def on_device(x, occupancy, wq, wk, wv, wo, cq, ck, cv, co, f1, f2, wp):
    x = x.reshape(ROWS, E)

    qkv, xr = row_proj(x, occupancy, wq, wk, wv)
    qkv = exchange(qkv, "cols")
    parts = exchange(partial_logits(qkv).reshape(N, I, SITES), "depth")
    px = exchange(row_softmax(parts, xr.reshape(N, I, XW)), "depth")
    mix = row_mix(px, qkv)
    mr = exchange(mix.reshape(N * N, 16, 128), ("cols", "depth")).reshape(4096, 128)

    both, right = column_step(mr, px, f1.T, f2.T, wo, cq, ck, cv, co)
    right = swap(right)
    both = exchange(both, "depth")
    counts = swap(both[:, I : I + 2, 512:640].reshape(C, 128))
    right = exchange(jnp.broadcast_to(right[None], (N, 2 * C, SEQS)), "cols")
    out = back(both)
    pair = pair_step(both, right, counts, wp)
    return out.reshape(S, I, E), pair.reshape(C, C, PC)


def solution(mesh):
    placed = (P("depth", "cols", None), P("depth", "cols")) + (P(),) * 11
    return jax.shard_map(
        on_device,
        mesh=mesh,
        in_specs=placed,
        out_specs=(P("depth", "cols", None), P("cols", "depth", None)),
        check_vma=False,
    )
```

```python
import functools
import math

import jax
import jax.numpy as jnp
from jax import lax
from jax.experimental import pallas as pl
from jax.experimental.pallas import tpu as pltpu
from jax.sharding import PartitionSpec as P

f32 = jnp.float32
bf16 = jnp.bfloat16

S = 16
I = 32
E = 768
H = 12
N = 16
ROWS = S * I
SEQS = 256
SITES = 512
C = 32
PC = 128
XW = E + 128
PARTS = 2

NT = (((1,), (1,)), ((), ()))


def norm(wide):
    center = wide - jnp.mean(wide, axis=-1, keepdims=True)
    spread = jnp.mean(center * center, axis=-1, keepdims=True)
    return (center * lax.rsqrt(spread + 1e-05)).astype(bf16)


def mm(a, b):
    return jnp.dot(a, b, preferred_element_type=f32)


def mmt(a, b):
    return lax.dot_general(a, b, NT, preferred_element_type=f32)


def lanes_lo(a, b):
    return jnp.concatenate([a[:, :64], b[:, :64]], axis=1)


def lanes_hi(a, b):
    return jnp.concatenate([a[:, 64:], b[:, 64:]], axis=1)


HBM = pl.BlockSpec(memory_space=pltpu.HBM)


def whole(n):
    return [pl.BlockSpec(memory_space=pltpu.VMEM)] * n


def params(mib):
    return pltpu.CompilerParams(vmem_limit_bytes=int(mib * 1024 * 1024))


def cost(flops, bytes_accessed, transcendentals=0):
    return pl.CostEstimate(
        flops=flops, bytes_accessed=bytes_accessed, transcendentals=transcendentals
    )


def mask_rows(occupancy, width):
    s = lax.broadcasted_iota(jnp.int32, (ROWS, S), 0) // I
    own = s == lax.broadcasted_iota(jnp.int32, (ROWS, S), 1)
    spread = mm(jnp.where(own, 1.0, 0.0).astype(bf16), occupancy.astype(f32).astype(bf16))
    i = lax.broadcasted_iota(jnp.int32, (ROWS, I), 0) % I
    own = i == lax.broadcasted_iota(jnp.int32, (ROWS, I), 1)
    column = jnp.sum(jnp.where(own, spread, 0.0), axis=-1, keepdims=True)
    return jnp.broadcast_to(column, (ROWS, width))


def row_proj_kernel(
    x_hbm, occ_hbm, wq_hbm, wk_hbm, wv_hbm, out_hbm,
    xv, occ, wv, xn_ref, out, sems,
):
    first = [pltpu.make_async_copy(occ_hbm, occ, sems.at[0])]
    for k in range(4):
        rows = pl.ds(128 * k, 128)
        first.append(pltpu.make_async_copy(x_hbm.at[rows], xv.at[rows], sems.at[1 + k]))
    for copy in first:
        copy.start()
    tiles = [
        pltpu.make_async_copy(w, wv.at[k], sems.at[5 + k])
        for k, w in enumerate((wq_hbm, wk_hbm, wv_hbm))
    ]
    first[0].wait()
    live = mask_rows(occ[...], 128)
    for k in range(4):
        first[1 + k].wait()
        if k == 0:
            tiles[0].start()
        rows = slice(128 * k, 128 * k + 128)
        xn_ref[rows] = norm(xv[rows].astype(f32))
    for copy in tiles[1:]:
        copy.start()
    sent = []
    xn = xn_ref[...]
    half = ROWS // 2
    for index in range(3):
        tiles[index].wait()
        rows = slice(256 * index, 256 * index + 256)
        for n in range(3):
            y = mm(xn, wv[index, :, 256 * n : 256 * n + 256])
            for t in range(2):
                part = y[:, 128 * t : 128 * t + 128]
                if index < 2:
                    part = part * live
                part = part.astype(bf16)
                a, b = part[:half], part[half:]
                out[4 * n + 2 * t, rows] = lanes_lo(a, b)
                out[4 * n + 2 * t + 1, rows] = lanes_hi(a, b)
        at = pl.ds(256 * index, 256)
        sent.append(
            pltpu.make_async_copy(
                out.at[:, at], out_hbm.at[pl.ds(0, H), at], sems.at[9 + index]
            )
        )
        sent[-1].start()
    for copy in sent:
        copy.wait()


def row_proj(x, occupancy, wq, wk, wv):
    return pl.pallas_call(
        row_proj_kernel,
        in_specs=[HBM] * 5,
        out_specs=HBM,
        out_shape=jax.ShapeDtypeStruct((N, 768, 128), bf16),
        scratch_shapes=[
            pltpu.VMEM((ROWS, E), bf16),
            pltpu.VMEM((S, I), jnp.int32),
            pltpu.VMEM((3, E, E), bf16),
            pltpu.VMEM((ROWS, E), bf16),
            pltpu.VMEM((H, 768, 128), bf16),
            pltpu.SemaphoreType.DMA((12,)),
        ],
        compiler_params=params(61),
        cost_estimate=cost(3 * 2 * ROWS * E * E, 8_000_000),
    )(x, occupancy, wq, wk, wv)


def turn_kernel(me_ref, x_ref, occ_ref, *out_refs):
    r = lax.broadcasted_iota(jnp.int32, (ROWS, ROWS), 0)
    o = lax.broadcasted_iota(jnp.int32, (ROWS, ROWS), 1)
    d = jnp.bitwise_xor(r >> 5, me_ref[0])
    src = ((r & 15) << 5) + (d << 1) + ((r >> 4) & 1)
    perm = jnp.where(src == o, 1.0, 0.0).astype(bf16)
    x = mm(perm, x_ref[...]).astype(bf16)
    mask = mm(perm, mask_rows(occ_ref[...], 128).astype(bf16)).astype(bf16)
    for k in range(N):
        out_refs[k][:, :E] = x[I * k : I * k + I]
        out_refs[k][:, E:] = mask[I * k : I * k + I]


def turn(me, x, occupancy):
    return pl.pallas_call(
        turn_kernel,
        in_specs=[pl.BlockSpec(memory_space=pltpu.SMEM)] + whole(2),
        out_specs=whole(N),
        out_shape=[jax.ShapeDtypeStruct((I, XW), bf16)] * N,
        compiler_params=params(16),
        cost_estimate=cost(2 * ROWS * ROWS * E, 3_000_000),
    )(me, x, occupancy)


def logits_kernel(qk_ref, out_ref):
    def side(k):
        return jnp.concatenate(
            [
                qk_ref[:, 256 * k + I * s : 256 * k + I * s + I, :].reshape(SITES, 128)
                for s in range(S // 2)
            ],
            axis=1,
        )

    out_ref[...] = mmt(side(0), side(1)) * (1.0 / math.sqrt(64 * SEQS))


def partial_logits(qkv):
    return pl.pallas_call(
        logits_kernel,
        grid=(1,),
        in_specs=[pl.BlockSpec((N, 512, 128), lambda n: (0, 0, 0))],
        out_specs=pl.BlockSpec((SITES, SITES), lambda n: (0, 0)),
        out_shape=jax.ShapeDtypeStruct((SITES, SITES), f32),
        compiler_params=params(20),
        cost_estimate=cost(2 * SITES * SITES * 1024, 3_000_000),
    )(qkv)


def softmax_kernel(in_ref, out_ref):
    total = in_ref[0]
    for k in range(1, N):
        total = total + in_ref[k]
    top = jnp.max(total, axis=-1, keepdims=True)
    e = jnp.exp(total - top)
    p = (e / jnp.sum(e, axis=-1, keepdims=True)).astype(bf16)
    for k in range(N):
        out_ref[k] = p


def row_softmax(parts):
    return pl.pallas_call(
        softmax_kernel,
        in_specs=whole(1),
        out_specs=pl.BlockSpec(memory_space=pltpu.VMEM),
        out_shape=jax.ShapeDtypeStruct((N, I, SITES), bf16),
        compiler_params=params(16),
        cost_estimate=cost(N * I * SITES, 4_000_000, I * SITES),
    )(parts)


def row_mix_kernel(p_ref, v_ref, out_ref):
    v = jnp.concatenate(
        [v_ref[:, I * s : I * s + I, :].reshape(SITES, 128) for s in range(S // 2)],
        axis=1,
    )
    mix = mm(p_ref[...].reshape(SITES, SITES), v).astype(bf16)
    r = lax.broadcasted_iota(jnp.int32, (256, 256), 0)
    o = lax.broadcasted_iota(jnp.int32, (256, 256), 1)
    perm = jnp.where(((r & 7) << 5) + (r >> 3) == o, 1.0, 0.0).astype(bf16)

    def block(b):
        part = mix[I * b : I * b + I, :]
        return jnp.concatenate(
            [part[:, 128 * s : 128 * s + 128] for s in range(8)], axis=0
        )

    for b in range(0, N, 2):
        pair = jnp.concatenate([block(b), block(b + 1)], axis=1)
        turned = mm(perm, pair).astype(bf16)
        out_ref[256 * b : 256 * b + 256, :] = turned[:, :128]
        out_ref[256 * b + 256 : 256 * b + 512, :] = turned[:, 128:]


def row_mix(p, qkv):
    return pl.pallas_call(
        row_mix_kernel,
        grid=(1,),
        in_specs=[
            pl.BlockSpec((N, I, SITES), lambda n: (0, 0, 0)),
            pl.BlockSpec((N, 256, 128), lambda n: (0, 2, 0)),
        ],
        out_specs=pl.BlockSpec((4096, 128), lambda n: (0, 0)),
        out_shape=jax.ShapeDtypeStruct((4096, 128), bf16),
        compiler_params=params(20),
        cost_estimate=cost(2 * SITES * SITES * 1024, 3_000_000),
    )(p, qkv)


def column_kernel(
    me_ref, mr_ref, f1_ref, f2_ref, wo_hbm, cq_hbm, ck_hbm, cv_hbm, co_hbm, *refs
):
    x_hbm, refs = refs[:N], refs[N:]
    out_hbm, r_ref, ysc, xsc, qs, ks, vs, ms, weights, xb, ao, left, sems, out_sems = refs
    copies = []
    for k, w in enumerate((wo_hbm, cq_hbm, ck_hbm, cv_hbm, co_hbm)):
        for part in range(PARTS):
            rows = pl.ds(E // PARTS * part, E // PARTS)
            copies.append(
                pltpu.make_async_copy(w.at[rows], weights.at[k, rows], sems.at[PARTS * k + part])
            )
    fetch = []
    for k in range(N):
        fetch.append(
            pltpu.make_async_copy(
                x_hbm[k], xb.at[jnp.bitwise_xor(me_ref[0], k)], sems.at[5 * PARTS + k]
            )
        )
    for copy in copies[:PARTS] + fetch + copies[PARTS:]:
        copy.start()

    def weight(k):
        for copy in copies[PARTS * k : PARTS * k + PARTS]:
            copy.wait()
        return weights[k]

    halves = []
    for pick in (lanes_lo, lanes_hi):
        halves.append(
            jnp.concatenate(
                [
                    pick(mr_ref[512 * t : 512 * t + 256, :], mr_ref[512 * t + 256 : 512 * t + 512, :])
                    for t in range(H // 2)
                ],
                axis=1,
            )
        )
    mixed = jnp.concatenate(halves, axis=0)
    ysc[...] = mm(mixed, weight(0)).reshape(2, N, 2, 8, E)
    for copy in fetch:
        copy.wait()
    xsc[...] = xb[...].astype(f32).reshape(N, 2, 2, 8, XW)
    blocks = []
    masks = []
    for i in range(2):
        for s2 in range(2):
            blocks.append((ysc[s2, :, i] + xsc[:, i, s2, :, :E]).reshape(128, E))
            masks.append(xsc[:, i, s2, :, E:].reshape(128, 128))
    after_rows = jnp.concatenate(blocks, axis=0).astype(bf16)
    wide = after_rows.astype(f32)
    mask = jnp.concatenate(masks, axis=0).astype(bf16)
    lane0 = jnp.where(
        lax.broadcasted_iota(jnp.int32, (8, 128), 1) == 0, 1.0, 0.0
    ).astype(bf16)
    alive = mmt(lane0, mask)

    normed = norm(wide)
    qs[...] = mm(normed, weight(1)).astype(bf16)
    ks[...] = mm(normed, weight(2)).astype(bf16)
    vs[...] = mm(normed, weight(3)).astype(bf16)
    low = lax.broadcasted_iota(jnp.int32, (SEQS, 128), 1) < 64
    for i in range(2):
        rows = slice(SEQS * i, SEQS * i + SEQS)
        keep = alive[0:1, rows] > 0
        for t in range(H // 2):
            lanes = slice(128 * t, 128 * t + 128)
            q, k, v = qs[rows, lanes], ks[rows, lanes], vs[rows, lanes]
            mixes = []
            for own in (low, jnp.logical_not(low)):
                logits = mmt(jnp.where(own, q, jnp.zeros_like(q)), k) * 0.125
                logits = jnp.where(keep, logits, -1000000000.0)
                e = jnp.exp(logits - jnp.max(logits, axis=-1, keepdims=True))
                p = (e * (1.0 / jnp.sum(e, axis=-1, keepdims=True))).astype(bf16)
                mixes.append(mm(p, v))
            ms[rows, lanes] = jnp.where(low, mixes[0], mixes[1]).astype(bf16)

    out = (wide + mm(ms[...], weight(4))).astype(bf16)
    out_wide = out.astype(f32)
    for i in range(2):
        for s2 in range(2):
            at = SEQS * i + 128 * s2
            xsc[:, i, s2, :, :E] = out_wide[at : at + 128].reshape(N, 8, E)
    ao[...] = xsc[:, :, :, :, :E].reshape(N, I, E).astype(bf16)
    sent = [pltpu.make_async_copy(ao, out_hbm.at[:, pl.ds(0, I)], out_sems.at[N])]
    sent[0].start()

    f = jnp.concatenate([f1_ref[...], f2_ref[...]], axis=0)
    factors = (mmt(f, norm(out_wide)) * alive[0:1, :]).astype(bf16)
    for i in range(2):
        r_ref[C * i : C * i + C, :] = factors[C:, SEQS * i : SEQS * i + SEQS]
    counts = [
        jnp.sum(alive[0:1, SEQS * i : SEQS * i + SEQS], axis=-1, keepdims=True)
        for i in range(2)
    ]
    row = lax.broadcasted_iota(jnp.int32, (C, SEQS), 0)
    count = jnp.where(row == 0, counts[0], counts[1]).astype(bf16)
    left[...] = jnp.concatenate([factors[:C, :], count], axis=1)
    for k in range(N):
        sent.append(pltpu.make_async_copy(left, out_hbm.at[k, pl.ds(I, C)], out_sems.at[k]))
        sent[-1].start()
    for copy in sent:
        copy.wait()


def column_step(me, mr, f1, f2, wo, cq, ck, cv, co, xs):
    return pl.pallas_call(
        column_kernel,
        in_specs=[pl.BlockSpec(memory_space=pltpu.SMEM)] + whole(3) + [HBM] * (5 + N),
        out_specs=[HBM, pl.BlockSpec(memory_space=pltpu.VMEM)],
        out_shape=[
            jax.ShapeDtypeStruct((N, 2 * I, E), bf16),
            jax.ShapeDtypeStruct((2 * C, SEQS), bf16),
        ],
        scratch_shapes=[
            pltpu.VMEM((2, N, 2, 8, E), f32),
            pltpu.VMEM((N, 2, 2, 8, XW), f32),
            pltpu.VMEM((ROWS, E), bf16),
            pltpu.VMEM((ROWS, E), bf16),
            pltpu.VMEM((ROWS, E), bf16),
            pltpu.VMEM((ROWS, E), bf16),
            pltpu.VMEM((5, E, E), bf16),
            pltpu.VMEM((N, I, XW), bf16),
            pltpu.VMEM((N, I, E), bf16),
            pltpu.VMEM((C, E), bf16),
            pltpu.SemaphoreType.DMA((5 * PARTS + N,)),
            pltpu.SemaphoreType.DMA((N + 1,)),
        ],
        compiler_params=params(59),
        cost_estimate=cost(5 * 2 * ROWS * E * E, 9_000_000, 2 * H * SEQS * SEQS),
    )(me, mr, f1, f2, wo, cq, ck, cv, co, *xs)


def back_kernel(in_ref, out_ref):
    o = lax.broadcasted_iota(jnp.int32, (ROWS, ROWS), 0)
    r = lax.broadcasted_iota(jnp.int32, (ROWS, ROWS), 1)
    src = (((o >> 1) & 15) << 5) + ((o & 1) << 4) + (o >> 5)
    perm = jnp.where(src == r, 1.0, 0.0).astype(bf16)
    out_ref[...] = mm(perm, in_ref[...].reshape(ROWS, E)).astype(bf16)


def back(both):
    return pl.pallas_call(
        back_kernel,
        grid=(1,),
        in_specs=[pl.BlockSpec((N, I, E), lambda n: (0, 0, 0))],
        out_specs=pl.BlockSpec((ROWS, E), lambda n: (0, 0)),
        out_shape=jax.ShapeDtypeStruct((ROWS, E), bf16),
        compiler_params=params(24),
        cost_estimate=cost(2 * ROWS * ROWS * E, 2_000_000),
    )(both)


def pair_kernel(
    l_ref, r_ref, n_ref, wp_ref, out_ref, l0, l1, l2, l3, l4, lp, lhs, osc, wk
):
    wk[...] = jnp.zeros_like(wk)
    for c in range(C):
        w = wp_ref[C * c : C * c + C, :]
        for j in range(4):
            at = 128 * c + C * j
            wk[at : at + C, 128 * j : 128 * j + 128] = w
    every = l_ref[...].reshape(N * C, E).astype(f32)
    for k, ref in enumerate((l0, l1, l2, l3, l4)):
        ref[...] = every[:, 128 * k : 128 * k + 128]

    def across(ref, row):
        return ref[pl.ds(row, N, stride=C), :]

    for c in range(C):
        rows = slice(C * c, C * c + C)
        lp[rows, :128] = jnp.concatenate([across(l0, c), across(l2, c)], axis=0).astype(bf16)
        lp[rows, 128:] = jnp.concatenate([across(l1, c), across(l3, c)], axis=0).astype(bf16)
    left_count = jnp.concatenate([across(l4, 0), across(l4, 1)], axis=0)
    right = r_ref[...].reshape(N * 2 * C, SEQS)
    for c in range(0, C, 4):
        outer = mmt(lp[C * c : C * c + 4 * C, :], right).astype(bf16)
        for k in range(4):
            for j in range(8):
                lhs[C * j : C * j + C, 128 * (c + k) : 128 * (c + k) + 128] = outer[
                    C * k : C * k + C, 128 * j : 128 * j + 128
                ]
    acc = mm(lhs[...], wk[...])
    right_count = n_ref[...].astype(f32)
    for j in range(C):
        part = acc[C * (j // 4) : C * (j // 4) + C, 128 * (j % 4) : 128 * (j % 4) + 128]
        part = part / (jnp.minimum(left_count, right_count[j : j + 1, :]) + 0.001)
        for i in range(2):
            osc[pl.ds(C * i + j, N, stride=2 * C), :] = part[N * i : N * i + N, :]
    out_ref[...] = osc[...].astype(bf16)


def pair_step(both, right, counts, wp):
    return pl.pallas_call(
        pair_kernel,
        grid=(1,),
        in_specs=[
            pl.BlockSpec((N, I, E), lambda n: (0, 1, 0)),
            pl.BlockSpec((N, 2 * C, SEQS), lambda n: (0, 0, 0)),
            pl.BlockSpec((C, 128), lambda n: (0, 0)),
            pl.BlockSpec((C * C, PC), lambda n: (0, 0)),
        ],
        out_specs=pl.BlockSpec((C * C, PC), lambda n: (0, 0)),
        out_shape=jax.ShapeDtypeStruct((C * C, PC), bf16),
        scratch_shapes=[pltpu.VMEM((N * C, 128), f32)] * 5
        + [
            pltpu.VMEM((1024, SEQS), bf16),
            pltpu.VMEM((256, 4096), bf16),
            pltpu.VMEM((1024, PC), f32),
            pltpu.VMEM((4096, 512), bf16),
        ],
        compiler_params=params(24),
        cost_estimate=cost(2 * 1024 * 1024 * 256 + 2 * 256 * 4096 * 512, 6_000_000),
    )(both, right, counts, wp)


def exchange(x, axis):
    return lax.all_to_all(x, axis, split_axis=0, concat_axis=0, tiled=True)


def swap(x):
    pairs = [(N * d + g, N * g + d) for d in range(N) for g in range(N)]
    return lax.ppermute(x, ("depth", "cols"), pairs)


def on_device(x, occupancy, wq, wk, wv, wo, cq, ck, cv, co, f1, f2, wp):
    x = x.reshape(ROWS, E)

    me = lax.axis_index("depth").astype(jnp.int32).reshape(1)

    sent = row_proj(x, occupancy, wq, wk, wv)
    qkv = exchange(sent, "cols")
    later, _ = lax.optimization_barrier((x, sent))
    xs = list(turn(me, later, occupancy))
    for k in range(1, N):
        xs[k] = lax.ppermute(xs[k], "depth", [(d, d ^ k) for d in range(N)])
    qkv, xs = lax.optimization_barrier((qkv, xs))

    parts = exchange(partial_logits(qkv).reshape(N, I, SITES), "depth")
    p = exchange(row_softmax(parts), "depth")
    mix = row_mix(p, qkv)
    mr = exchange(mix.reshape(N * N, 16, 128), ("cols", "depth")).reshape(4096, 128)

    both, right = column_step(me, mr, f1.T, f2.T, wo, cq, ck, cv, co, xs)
    right = swap(right)
    both = exchange(both, "depth")
    counts = swap(both[:, I : I + 2, 512:640].reshape(C, 128))
    right = exchange(jnp.broadcast_to(right[None], (N, 2 * C, SEQS)), "cols")
    out = back(both)
    pair = pair_step(both, right, counts, wp)
    return out.reshape(S, I, E), pair.reshape(C, C, PC)


def solution(mesh):
    placed = (P("depth", "cols", None), P("depth", "cols")) + (P(),) * 11
    return jax.shard_map(
        on_device,
        mesh=mesh,
        in_specs=placed,
        out_specs=(P("depth", "cols", None), P("cols", "depth", None)),
        check_vma=False,
    )
```

```python
import functools
import math

import jax
import jax.numpy as jnp
from jax import lax
from jax.experimental import pallas as pl
from jax.experimental.pallas import tpu as pltpu
from jax.sharding import PartitionSpec as P

f32 = jnp.float32
bf16 = jnp.bfloat16

S = 16
I = 32
E = 768
H = 12
N = 16
ROWS = S * I
SEQS = 256
SITES = 512
C = 32
PC = 128
XW = E + 128
RW = 80
PARTS = 2

NT = (((1,), (1,)), ((), ()))


def norm(wide):
    center = wide - jnp.mean(wide, axis=-1, keepdims=True)
    spread = jnp.mean(center * center, axis=-1, keepdims=True)
    return (center * lax.rsqrt(spread + 1e-05)).astype(bf16)


def mm(a, b):
    return jnp.dot(a, b, preferred_element_type=f32)


def mmt(a, b):
    return lax.dot_general(a, b, NT, preferred_element_type=f32)


def lanes_lo(a, b):
    return jnp.concatenate([a[:, :64], b[:, :64]], axis=1)


def lanes_hi(a, b):
    return jnp.concatenate([a[:, 64:], b[:, 64:]], axis=1)


HBM = pl.BlockSpec(memory_space=pltpu.HBM)


def whole(n):
    return [pl.BlockSpec(memory_space=pltpu.VMEM)] * n


def params(mib):
    return pltpu.CompilerParams(vmem_limit_bytes=int(mib * 1024 * 1024))


def cost(flops, bytes_accessed, transcendentals=0):
    return pl.CostEstimate(
        flops=flops, bytes_accessed=bytes_accessed, transcendentals=transcendentals
    )


def mask_rows(occupancy, width):
    s = lax.broadcasted_iota(jnp.int32, (ROWS, S), 0) // I
    own = s == lax.broadcasted_iota(jnp.int32, (ROWS, S), 1)
    spread = mm(jnp.where(own, 1.0, 0.0).astype(bf16), occupancy.astype(f32).astype(bf16))
    i = lax.broadcasted_iota(jnp.int32, (ROWS, I), 0) % I
    own = i == lax.broadcasted_iota(jnp.int32, (ROWS, I), 1)
    column = jnp.sum(jnp.where(own, spread, 0.0), axis=-1, keepdims=True)
    return jnp.broadcast_to(column, (ROWS, width))


def row_proj_kernel(
    x_hbm, occ_hbm, wq_hbm, wk_hbm, wv_hbm, out_hbm,
    xv, occ, wv, xn_ref, out, sems,
):
    first = [pltpu.make_async_copy(occ_hbm, occ, sems.at[0])]
    for k in range(4):
        rows = pl.ds(128 * k, 128)
        first.append(pltpu.make_async_copy(x_hbm.at[rows], xv.at[rows], sems.at[1 + k]))
    for copy in first:
        copy.start()
    tiles = [
        pltpu.make_async_copy(w, wv.at[k], sems.at[5 + k])
        for k, w in enumerate((wq_hbm, wk_hbm, wv_hbm))
    ]
    first[0].wait()
    live = mask_rows(occ[...], 128)
    for k in range(4):
        first[1 + k].wait()
        if k == 0:
            tiles[0].start()
        rows = slice(128 * k, 128 * k + 128)
        xn_ref[rows] = norm(xv[rows].astype(f32))
    for copy in tiles[1:]:
        copy.start()
    sent = []
    xn = xn_ref[...]
    half = ROWS // 2
    for index in range(3):
        tiles[index].wait()
        rows = slice(256 * index, 256 * index + 256)
        for n in range(3):
            y = mm(xn, wv[index, :, 256 * n : 256 * n + 256])
            for t in range(2):
                part = y[:, 128 * t : 128 * t + 128]
                if index < 2:
                    part = part * live
                part = part.astype(bf16)
                a, b = part[:half], part[half:]
                out[4 * n + 2 * t, rows] = lanes_lo(a, b)
                out[4 * n + 2 * t + 1, rows] = lanes_hi(a, b)
        at = pl.ds(256 * index, 256)
        sent.append(
            pltpu.make_async_copy(
                out.at[:, at], out_hbm.at[pl.ds(0, H), at], sems.at[9 + index]
            )
        )
        sent[-1].start()
    for copy in sent:
        copy.wait()


def row_proj(x, occupancy, wq, wk, wv):
    return pl.pallas_call(
        row_proj_kernel,
        in_specs=[HBM] * 5,
        out_specs=HBM,
        out_shape=jax.ShapeDtypeStruct((N, 768, 128), bf16),
        scratch_shapes=[
            pltpu.VMEM((ROWS, E), bf16),
            pltpu.VMEM((S, I), jnp.int32),
            pltpu.VMEM((3, E, E), bf16),
            pltpu.VMEM((ROWS, E), bf16),
            pltpu.VMEM((H, 768, 128), bf16),
            pltpu.SemaphoreType.DMA((12,)),
        ],
        compiler_params=params(61),
        cost_estimate=cost(3 * 2 * ROWS * E * E, 8_000_000),
    )(x, occupancy, wq, wk, wv)


def turn_kernel(me_ref, x_ref, occ_ref, *out_refs):
    r = lax.broadcasted_iota(jnp.int32, (ROWS, ROWS), 0)
    o = lax.broadcasted_iota(jnp.int32, (ROWS, ROWS), 1)
    d = jnp.bitwise_xor(r >> 5, me_ref[0])
    src = ((r & 15) << 5) + (d << 1) + ((r >> 4) & 1)
    perm = jnp.where(src == o, 1.0, 0.0).astype(bf16)
    x = mm(perm, x_ref[...]).astype(bf16)
    mask = mm(perm, mask_rows(occ_ref[...], 128).astype(bf16)).astype(bf16)
    for k in range(N):
        out_refs[k][:, :E] = x[I * k : I * k + I]
        out_refs[k][:, E:] = mask[I * k : I * k + I]


def turn(me, x, occupancy):
    return pl.pallas_call(
        turn_kernel,
        in_specs=[pl.BlockSpec(memory_space=pltpu.SMEM)] + whole(2),
        out_specs=whole(N),
        out_shape=[jax.ShapeDtypeStruct((I, XW), bf16)] * N,
        compiler_params=params(16),
        cost_estimate=cost(2 * ROWS * ROWS * E, 3_000_000),
    )(me, x, occupancy)


def logits_kernel(qk_ref, out_ref):
    def side(k):
        return jnp.concatenate(
            [
                qk_ref[:, 256 * k + I * s : 256 * k + I * s + I, :].reshape(SITES, 128)
                for s in range(S // 2)
            ],
            axis=1,
        )

    out_ref[...] = (mmt(side(0), side(1)) * (1.0 / math.sqrt(64 * SEQS))).astype(bf16)


def partial_logits(qkv):
    return pl.pallas_call(
        logits_kernel,
        grid=(1,),
        in_specs=[pl.BlockSpec((N, 512, 128), lambda n: (0, 0, 0))],
        out_specs=pl.BlockSpec((SITES, SITES), lambda n: (0, 0)),
        out_shape=jax.ShapeDtypeStruct((SITES, SITES), bf16),
        compiler_params=params(20),
        cost_estimate=cost(2 * SITES * SITES * 1024, 3_000_000),
    )(qkv)


def softmax_kernel(in_ref, out_ref):
    total = in_ref[0].astype(f32)
    for k in range(1, N):
        total = total + in_ref[k].astype(f32)
    top = jnp.max(total, axis=-1, keepdims=True)
    e = jnp.exp(total - top)
    p = (e / jnp.sum(e, axis=-1, keepdims=True)).astype(bf16)
    for k in range(N):
        out_ref[k] = p


def row_softmax(parts):
    return pl.pallas_call(
        softmax_kernel,
        in_specs=whole(1),
        out_specs=pl.BlockSpec(memory_space=pltpu.VMEM),
        out_shape=jax.ShapeDtypeStruct((N, I, SITES), bf16),
        compiler_params=params(16),
        cost_estimate=cost(N * I * SITES, 4_000_000, I * SITES),
    )(parts)


def row_mix_kernel(p_ref, v_ref, out_ref):
    v = jnp.concatenate(
        [v_ref[:, I * s : I * s + I, :].reshape(SITES, 128) for s in range(S // 2)],
        axis=1,
    )
    mix = mm(p_ref[...].reshape(SITES, SITES), v).astype(bf16)
    r = lax.broadcasted_iota(jnp.int32, (256, 256), 0)
    o = lax.broadcasted_iota(jnp.int32, (256, 256), 1)
    perm = jnp.where(((r & 7) << 5) + (r >> 3) == o, 1.0, 0.0).astype(bf16)

    def block(b):
        part = mix[I * b : I * b + I, :]
        return jnp.concatenate(
            [part[:, 128 * s : 128 * s + 128] for s in range(8)], axis=0
        )

    for b in range(0, N, 2):
        pair = jnp.concatenate([block(b), block(b + 1)], axis=1)
        turned = mm(perm, pair).astype(bf16)
        out_ref[256 * b : 256 * b + 256, :] = turned[:, :128]
        out_ref[256 * b + 256 : 256 * b + 512, :] = turned[:, 128:]


def row_mix(p, qkv):
    return pl.pallas_call(
        row_mix_kernel,
        grid=(1,),
        in_specs=[
            pl.BlockSpec((N, I, SITES), lambda n: (0, 0, 0)),
            pl.BlockSpec((N, 256, 128), lambda n: (0, 2, 0)),
        ],
        out_specs=pl.BlockSpec((4096, 128), lambda n: (0, 0)),
        out_shape=jax.ShapeDtypeStruct((4096, 128), bf16),
        compiler_params=params(20),
        cost_estimate=cost(2 * SITES * SITES * 1024, 3_000_000),
    )(p, qkv)


def column_kernel(
    me_ref, mr_ref, f1_ref, f2_ref, wo_hbm, cq_hbm, ck_hbm, cv_hbm, co_hbm, *refs
):
    x_hbm, refs = refs[:N], refs[N:]
    out_hbm, r_ref, ysc, xsc, qs, ks, vs, ms, weights, xb, ao, left, sems, out_sems = refs
    copies = []
    for k, w in enumerate((wo_hbm, cq_hbm, ck_hbm, cv_hbm, co_hbm)):
        for part in range(PARTS):
            rows = pl.ds(E // PARTS * part, E // PARTS)
            copies.append(
                pltpu.make_async_copy(w.at[rows], weights.at[k, rows], sems.at[PARTS * k + part])
            )
    fetch = []
    for k in range(N):
        fetch.append(
            pltpu.make_async_copy(
                x_hbm[k], xb.at[jnp.bitwise_xor(me_ref[0], k)], sems.at[5 * PARTS + k]
            )
        )
    for copy in copies[:PARTS] + fetch + copies[PARTS:]:
        copy.start()

    def weight(k):
        for copy in copies[PARTS * k : PARTS * k + PARTS]:
            copy.wait()
        return weights[k]

    halves = []
    for pick in (lanes_lo, lanes_hi):
        halves.append(
            jnp.concatenate(
                [
                    pick(mr_ref[512 * t : 512 * t + 256, :], mr_ref[512 * t + 256 : 512 * t + 512, :])
                    for t in range(H // 2)
                ],
                axis=1,
            )
        )
    mixed = jnp.concatenate(halves, axis=0)
    ysc[...] = mm(mixed, weight(0)).reshape(2, N, 2, 8, E)
    for copy in fetch:
        copy.wait()
    xsc[...] = xb[...].astype(f32).reshape(N, 2, 2, 8, XW)
    blocks = []
    masks = []
    for i in range(2):
        for s2 in range(2):
            blocks.append((ysc[s2, :, i] + xsc[:, i, s2, :, :E]).reshape(128, E))
            masks.append(xsc[:, i, s2, :, E:].reshape(128, 128))
    after_rows = jnp.concatenate(blocks, axis=0).astype(bf16)
    wide = after_rows.astype(f32)
    mask = jnp.concatenate(masks, axis=0).astype(bf16)
    lane0 = jnp.where(
        lax.broadcasted_iota(jnp.int32, (8, 128), 1) == 0, 1.0, 0.0
    ).astype(bf16)
    alive = mmt(lane0, mask)

    normed = norm(wide)
    qs[...] = mm(normed, weight(1)).astype(bf16)
    ks[...] = mm(normed, weight(2)).astype(bf16)
    vs[...] = mm(normed, weight(3)).astype(bf16)
    low = lax.broadcasted_iota(jnp.int32, (SEQS, 128), 1) < 64
    for i in range(2):
        rows = slice(SEQS * i, SEQS * i + SEQS)
        keep = alive[0:1, rows] > 0
        for t in range(H // 2):
            lanes = slice(128 * t, 128 * t + 128)
            q, k, v = qs[rows, lanes], ks[rows, lanes], vs[rows, lanes]
            mixes = []
            for own in (low, jnp.logical_not(low)):
                logits = mmt(jnp.where(own, q, jnp.zeros_like(q)), k) * 0.125
                logits = jnp.where(keep, logits, -1000000000.0)
                e = jnp.exp(logits - jnp.max(logits, axis=-1, keepdims=True))
                p = (e * (1.0 / jnp.sum(e, axis=-1, keepdims=True))).astype(bf16)
                mixes.append(mm(p, v))
            ms[rows, lanes] = jnp.where(low, mixes[0], mixes[1]).astype(bf16)

    out = (wide + mm(ms[...], weight(4))).astype(bf16)
    out_wide = out.astype(f32)
    for i in range(2):
        for s2 in range(2):
            at = SEQS * i + 128 * s2
            xsc[:, i, s2, :, :E] = out_wide[at : at + 128].reshape(N, 8, E)
    ao[...] = xsc[:, :, :, :, :E].reshape(N, I, E).astype(bf16)
    sent = [pltpu.make_async_copy(ao, out_hbm.at[:, pl.ds(0, I)], out_sems.at[N])]
    sent[0].start()

    f = jnp.concatenate([f1_ref[...], f2_ref[...]], axis=0)
    factors = (mmt(f, norm(out_wide)) * alive[0:1, :]).astype(bf16)
    for i in range(2):
        r_ref[C * i : C * i + C, :] = factors[C:, SEQS * i : SEQS * i + SEQS]
    counts = [
        jnp.sum(alive[0:1, SEQS * i : SEQS * i + SEQS], axis=-1, keepdims=True)
        for i in range(2)
    ]
    row = lax.broadcasted_iota(jnp.int32, (C, SEQS), 0)
    count = jnp.where(row == 0, counts[0], counts[1]).astype(bf16)
    r_ref[2 * C :, :] = count[: RW - 2 * C, :]
    left[...] = jnp.concatenate([factors[:C, :], count], axis=1)
    for k in range(N):
        sent.append(pltpu.make_async_copy(left, out_hbm.at[k, pl.ds(I, C)], out_sems.at[k]))
        sent[-1].start()
    for copy in sent:
        copy.wait()


def column_step(me, mr, f1, f2, wo, cq, ck, cv, co, xs):
    return pl.pallas_call(
        column_kernel,
        in_specs=[pl.BlockSpec(memory_space=pltpu.SMEM)] + whole(3) + [HBM] * (5 + N),
        out_specs=[HBM, pl.BlockSpec(memory_space=pltpu.VMEM)],
        out_shape=[
            jax.ShapeDtypeStruct((N, 2 * I, E), bf16),
            jax.ShapeDtypeStruct((RW, SEQS), bf16),
        ],
        scratch_shapes=[
            pltpu.VMEM((2, N, 2, 8, E), f32),
            pltpu.VMEM((N, 2, 2, 8, XW), f32),
            pltpu.VMEM((ROWS, E), bf16),
            pltpu.VMEM((ROWS, E), bf16),
            pltpu.VMEM((ROWS, E), bf16),
            pltpu.VMEM((ROWS, E), bf16),
            pltpu.VMEM((5, E, E), bf16),
            pltpu.VMEM((N, I, XW), bf16),
            pltpu.VMEM((N, I, E), bf16),
            pltpu.VMEM((C, E), bf16),
            pltpu.SemaphoreType.DMA((5 * PARTS + N,)),
            pltpu.SemaphoreType.DMA((N + 1,)),
        ],
        compiler_params=params(59),
        cost_estimate=cost(5 * 2 * ROWS * E * E, 9_000_000, 2 * H * SEQS * SEQS),
    )(me, mr, f1, f2, wo, cq, ck, cv, co, *xs)


def back_kernel(in_ref, out_ref):
    o = lax.broadcasted_iota(jnp.int32, (ROWS, ROWS), 0)
    r = lax.broadcasted_iota(jnp.int32, (ROWS, ROWS), 1)
    src = (((o >> 1) & 15) << 5) + ((o & 1) << 4) + (o >> 5)
    perm = jnp.where(src == r, 1.0, 0.0).astype(bf16)
    out_ref[...] = mm(perm, in_ref[...].reshape(ROWS, E)).astype(bf16)


def back(both):
    return pl.pallas_call(
        back_kernel,
        grid=(1,),
        in_specs=[pl.BlockSpec((N, I, E), lambda n: (0, 0, 0))],
        out_specs=pl.BlockSpec((ROWS, E), lambda n: (0, 0)),
        out_shape=jax.ShapeDtypeStruct((ROWS, E), bf16),
        compiler_params=params(24),
        cost_estimate=cost(2 * ROWS * ROWS * E, 2_000_000),
    )(both)


def pair_kernel(
    me_ref, l_ref, r0, r1, r2, r3, wp_ref, out_ref,
    l0, l1, l2, l3, l4, lp, lhs, osc, wk, r_ref,
):
    for near, ref in enumerate((r0, r1, r2, r3)):
        for far in range(4):
            r_ref[jnp.bitwise_xor(me_ref[1], 4 * far + near)] = ref[RW * far : RW * far + RW]
    wk[...] = jnp.zeros_like(wk)
    for c in range(C):
        w = wp_ref[C * c : C * c + C, :]
        for j in range(4):
            at = 128 * c + C * j
            wk[at : at + C, 128 * j : 128 * j + 128] = w
    every = l_ref[...].reshape(N * C, E).astype(f32)
    for k, ref in enumerate((l0, l1, l2, l3, l4)):
        ref[...] = every[:, 128 * k : 128 * k + 128]

    def across(ref, row):
        return ref[pl.ds(row, N, stride=C), :]

    for c in range(C):
        rows = slice(C * c, C * c + C)
        lp[rows, :128] = jnp.concatenate([across(l0, c), across(l2, c)], axis=0).astype(bf16)
        lp[rows, 128:] = jnp.concatenate([across(l1, c), across(l3, c)], axis=0).astype(bf16)
    left_count = jnp.concatenate([across(l4, 0), across(l4, 1)], axis=0)
    right = r_ref[:, : 2 * C, :].reshape(N * 2 * C, SEQS)
    for c in range(0, C, 4):
        outer = mmt(lp[C * c : C * c + 4 * C, :], right).astype(bf16)
        for k in range(4):
            for j in range(8):
                lhs[C * j : C * j + C, 128 * (c + k) : 128 * (c + k) + 128] = outer[
                    C * k : C * k + C, 128 * j : 128 * j + 128
                ]
    acc = mm(lhs[...], wk[...])
    right_count = r_ref[:, 2 * C :, :128].astype(f32)
    for j in range(C):
        part = acc[C * (j // 4) : C * (j // 4) + C, 128 * (j % 4) : 128 * (j % 4) + 128]
        count = right_count[j // 2, j % 2 : j % 2 + 1, :]
        part = part / (jnp.minimum(left_count, count) + 0.001)
        for i in range(2):
            osc[pl.ds(C * i + j, N, stride=2 * C), :] = part[N * i : N * i + N, :]
    out_ref[...] = osc[...].astype(bf16)


def pair_step(me, both, rights, wp):
    return pl.pallas_call(
        pair_kernel,
        grid=(1,),
        in_specs=[
            pl.BlockSpec(memory_space=pltpu.SMEM),
            pl.BlockSpec((N, I, E), lambda n: (0, 1, 0)),
        ]
        + [pl.BlockSpec((4 * RW, SEQS), lambda n: (0, 0))] * 4
        + [pl.BlockSpec((C * C, PC), lambda n: (0, 0))],
        out_specs=pl.BlockSpec((C * C, PC), lambda n: (0, 0)),
        out_shape=jax.ShapeDtypeStruct((C * C, PC), bf16),
        scratch_shapes=[pltpu.VMEM((N * C, 128), f32)] * 5
        + [
            pltpu.VMEM((1024, SEQS), bf16),
            pltpu.VMEM((256, 4096), bf16),
            pltpu.VMEM((1024, PC), f32),
            pltpu.VMEM((4096, 512), bf16),
            pltpu.VMEM((N, RW, SEQS), bf16),
        ],
        compiler_params=params(24),
        cost_estimate=cost(2 * 1024 * 1024 * 256 + 2 * 256 * 4096 * 512, 6_000_000),
    )(me, both, *rights, wp)


def exchange(x, axis):
    return lax.all_to_all(x, axis, split_axis=0, concat_axis=0, tiled=True)


def swap(x):
    pairs = [(N * d + g, N * g + d) for d in range(N) for g in range(N)]
    return lax.ppermute(x, ("depth", "cols"), pairs)


def mirror(x, k, axis):
    return lax.ppermute(x, axis, [(d, d ^ k) for d in range(N)])


def on_device(x, occupancy, wq, wk, wv, wo, cq, ck, cv, co, f1, f2, wp):
    x = x.reshape(ROWS, E)

    me = jnp.stack([lax.axis_index("depth"), lax.axis_index("cols")]).astype(jnp.int32)

    sent = row_proj(x, occupancy, wq, wk, wv)
    qkv = exchange(sent, "cols")
    later, _ = lax.optimization_barrier((x, sent))
    xs = list(turn(me, later, occupancy))
    for k in range(1, N):
        xs[k] = mirror(xs[k], k, "depth")
    qkv, xs = lax.optimization_barrier((qkv, xs))

    parts = exchange(partial_logits(qkv).reshape(N, I, SITES), "depth")
    p = exchange(row_softmax(parts), "depth")
    mix = row_mix(p, qkv)
    mr = exchange(mix.reshape(N * N, 16, 128), ("cols", "depth")).reshape(4096, 128)

    both, right = column_step(me, mr, f1.T, f2.T, wo, cq, ck, cv, co, xs)
    both = exchange(both, "depth")
    right = swap(right)
    far = [right] + [mirror(right, 4 * k, "cols") for k in range(1, 4)]
    far = jnp.concatenate(far, axis=0)
    rights = [far] + [mirror(far, k, "cols") for k in range(1, 4)]
    out = back(both)
    pair = pair_step(me, both, rights, wp)
    return out.reshape(S, I, E), pair.reshape(C, C, PC)


def solution(mesh):
    placed = (P("depth", "cols", None), P("depth", "cols")) + (P(),) * 11
    return jax.shard_map(
        on_device,
        mesh=mesh,
        in_specs=placed,
        out_specs=(P("depth", "cols", None), P("cols", "depth", None)),
        check_vma=False,
    )
```

```python
import functools
import math

import jax
import jax.numpy as jnp
from jax import lax
from jax.experimental import pallas as pl
from jax.experimental.pallas import tpu as pltpu
from jax.sharding import PartitionSpec as P

f32 = jnp.float32
bf16 = jnp.bfloat16

S = 16
I = 32
E = 768
H = 12
N = 16
ROWS = S * I
SEQS = 256
SITES = 512
C = 32
PC = 128
XW = E + 128
RW = 80
PARTS = 2

NT = (((1,), (1,)), ((), ()))


def norm(wide):
    center = wide - jnp.mean(wide, axis=-1, keepdims=True)
    spread = jnp.mean(center * center, axis=-1, keepdims=True)
    return (center * lax.rsqrt(spread + 1e-05)).astype(bf16)


def mm(a, b):
    return jnp.dot(a, b, preferred_element_type=f32)


def mmt(a, b):
    return lax.dot_general(a, b, NT, preferred_element_type=f32)


def lanes_lo(a, b):
    return jnp.concatenate([a[:, :64], b[:, :64]], axis=1)


def lanes_hi(a, b):
    return jnp.concatenate([a[:, 64:], b[:, 64:]], axis=1)


HBM = pl.BlockSpec(memory_space=pltpu.HBM)


def whole(n):
    return [pl.BlockSpec(memory_space=pltpu.VMEM)] * n


def params(mib):
    return pltpu.CompilerParams(vmem_limit_bytes=int(mib * 1024 * 1024))


def cost(flops, bytes_accessed, transcendentals=0):
    return pl.CostEstimate(
        flops=flops, bytes_accessed=bytes_accessed, transcendentals=transcendentals
    )


def mask_rows(occupancy, width):
    s = lax.broadcasted_iota(jnp.int32, (ROWS, S), 0) // I
    own = s == lax.broadcasted_iota(jnp.int32, (ROWS, S), 1)
    spread = mm(jnp.where(own, 1.0, 0.0).astype(bf16), occupancy.astype(f32).astype(bf16))
    i = lax.broadcasted_iota(jnp.int32, (ROWS, I), 0) % I
    own = i == lax.broadcasted_iota(jnp.int32, (ROWS, I), 1)
    column = jnp.sum(jnp.where(own, spread, 0.0), axis=-1, keepdims=True)
    return jnp.broadcast_to(column, (ROWS, width))


def row_proj_kernel(
    x_hbm, occ_hbm, wq_hbm, wk_hbm, wv_hbm, out_hbm,
    xv, occ, wv, xn_ref, out, sems,
):
    first = [pltpu.make_async_copy(occ_hbm, occ, sems.at[0])]
    for k in range(4):
        rows = pl.ds(128 * k, 128)
        first.append(pltpu.make_async_copy(x_hbm.at[rows], xv.at[rows], sems.at[1 + k]))
    for copy in first:
        copy.start()
    tiles = [
        pltpu.make_async_copy(w, wv.at[k], sems.at[5 + k])
        for k, w in enumerate((wq_hbm, wk_hbm, wv_hbm))
    ]
    first[0].wait()
    live = mask_rows(occ[...], 128)
    for k in range(4):
        first[1 + k].wait()
        if k == 0:
            tiles[0].start()
        rows = slice(128 * k, 128 * k + 128)
        xn_ref[rows] = norm(xv[rows].astype(f32))
    for copy in tiles[1:]:
        copy.start()
    sent = []
    xn = xn_ref[...]
    half = ROWS // 2
    for copy in tiles:
        copy.wait()
    for index in range(3):
        rows = slice(256 * index, 256 * index + 256)
        for n in range(3):
            y = mm(xn, wv[index, :, 256 * n : 256 * n + 256])
            for t in range(2):
                part = y[:, 128 * t : 128 * t + 128]
                if index < 2:
                    part = part * live
                part = part.astype(bf16)
                a, b = part[:half], part[half:]
                out[4 * n + 2 * t, rows] = lanes_lo(a, b)
                out[4 * n + 2 * t + 1, rows] = lanes_hi(a, b)
        at = pl.ds(256 * index, 256)
        sent.append(
            pltpu.make_async_copy(
                out.at[:, at], out_hbm.at[pl.ds(0, H), at], sems.at[9 + index]
            )
        )
        sent[-1].start()
    for copy in sent:
        copy.wait()


def row_proj(x, occupancy, wq, wk, wv):
    return pl.pallas_call(
        row_proj_kernel,
        in_specs=[HBM] * 5,
        out_specs=HBM,
        out_shape=jax.ShapeDtypeStruct((N, 768, 128), bf16),
        scratch_shapes=[
            pltpu.VMEM((ROWS, E), bf16),
            pltpu.VMEM((S, I), jnp.int32),
            pltpu.VMEM((3, E, E), bf16),
            pltpu.VMEM((ROWS, E), bf16),
            pltpu.VMEM((H, 768, 128), bf16),
            pltpu.SemaphoreType.DMA((12,)),
        ],
        compiler_params=params(61),
        cost_estimate=cost(3 * 2 * ROWS * E * E, 8_000_000),
    )(x, occupancy, wq, wk, wv)


def turn_kernel(me_ref, x_ref, occ_ref, *out_refs):
    r = lax.broadcasted_iota(jnp.int32, (ROWS, ROWS), 0)
    o = lax.broadcasted_iota(jnp.int32, (ROWS, ROWS), 1)
    d = jnp.bitwise_xor(r >> 5, me_ref[0])
    src = ((r & 15) << 5) + (d << 1) + ((r >> 4) & 1)
    perm = jnp.where(src == o, 1.0, 0.0).astype(bf16)
    x = mm(perm, x_ref[...]).astype(bf16)
    mask = mm(perm, mask_rows(occ_ref[...], 128).astype(bf16)).astype(bf16)
    for k in range(N):
        out_refs[k][:, :E] = x[I * k : I * k + I]
        out_refs[k][:, E:] = mask[I * k : I * k + I]


def turn(me, x, occupancy):
    return pl.pallas_call(
        turn_kernel,
        in_specs=[pl.BlockSpec(memory_space=pltpu.SMEM)] + whole(2),
        out_specs=whole(N),
        out_shape=[jax.ShapeDtypeStruct((I, XW), bf16)] * N,
        compiler_params=params(16),
        cost_estimate=cost(2 * ROWS * ROWS * E, 3_000_000),
    )(me, x, occupancy)


def logits_kernel(qk_ref, out_ref):
    def side(k):
        return jnp.concatenate(
            [
                qk_ref[:, 256 * k + I * s : 256 * k + I * s + I, :].reshape(SITES, 128)
                for s in range(S // 2)
            ],
            axis=1,
        )

    out_ref[...] = (mmt(side(0), side(1)) * (1.0 / math.sqrt(64 * SEQS))).astype(bf16)


def partial_logits(qkv):
    return pl.pallas_call(
        logits_kernel,
        grid=(1,),
        in_specs=[pl.BlockSpec((N, 512, 128), lambda n: (0, 0, 0))],
        out_specs=pl.BlockSpec((SITES, SITES), lambda n: (0, 0)),
        out_shape=jax.ShapeDtypeStruct((SITES, SITES), bf16),
        compiler_params=params(20),
        cost_estimate=cost(2 * SITES * SITES * 1024, 3_000_000),
    )(qkv)


def softmax_kernel(in_ref, out_ref):
    total = in_ref[0].astype(f32)
    for k in range(1, N):
        total = total + in_ref[k].astype(f32)
    top = jnp.max(total, axis=-1, keepdims=True)
    e = jnp.exp(total - top)
    p = (e / jnp.sum(e, axis=-1, keepdims=True)).astype(bf16)
    for k in range(N):
        out_ref[k] = p


def row_softmax(parts):
    return pl.pallas_call(
        softmax_kernel,
        in_specs=whole(1),
        out_specs=pl.BlockSpec(memory_space=pltpu.VMEM),
        out_shape=jax.ShapeDtypeStruct((N, I, SITES), bf16),
        compiler_params=params(16),
        cost_estimate=cost(N * I * SITES, 4_000_000, I * SITES),
    )(parts)


def row_mix_kernel(p_ref, v_ref, out_ref):
    v = jnp.concatenate(
        [v_ref[:, I * s : I * s + I, :].reshape(SITES, 128) for s in range(S // 2)],
        axis=1,
    )
    mix = mm(p_ref[...].reshape(SITES, SITES), v).astype(bf16)
    r = lax.broadcasted_iota(jnp.int32, (256, 256), 0)
    o = lax.broadcasted_iota(jnp.int32, (256, 256), 1)
    perm = jnp.where(((r & 7) << 5) + (r >> 3) == o, 1.0, 0.0).astype(bf16)

    def block(b):
        part = mix[I * b : I * b + I, :]
        return jnp.concatenate(
            [part[:, 128 * s : 128 * s + 128] for s in range(8)], axis=0
        )

    for b in range(0, N, 2):
        pair = jnp.concatenate([block(b), block(b + 1)], axis=1)
        turned = mm(perm, pair).astype(bf16)
        out_ref[256 * b : 256 * b + 256, :] = turned[:, :128]
        out_ref[256 * b + 256 : 256 * b + 512, :] = turned[:, 128:]


def row_mix(p, qkv):
    return pl.pallas_call(
        row_mix_kernel,
        grid=(1,),
        in_specs=[
            pl.BlockSpec((N, I, SITES), lambda n: (0, 0, 0)),
            pl.BlockSpec((N, 256, 128), lambda n: (0, 2, 0)),
        ],
        out_specs=pl.BlockSpec((4096, 128), lambda n: (0, 0)),
        out_shape=jax.ShapeDtypeStruct((4096, 128), bf16),
        compiler_params=params(20),
        cost_estimate=cost(2 * SITES * SITES * 1024, 3_000_000),
    )(p, qkv)


def column_kernel(
    me_ref, mr_ref, f1_ref, f2_ref, wo_hbm, cq_hbm, ck_hbm, cv_hbm, co_hbm, *refs
):
    x_hbm, refs = refs[:N], refs[N:]
    out_ref, r_ref, ysc, xsc, qs, ks, vs, ms, weights, xb, sems = refs
    copies = []
    for k, w in enumerate((wo_hbm, cq_hbm, ck_hbm, cv_hbm, co_hbm)):
        for part in range(PARTS):
            rows = pl.ds(E // PARTS * part, E // PARTS)
            copies.append(
                pltpu.make_async_copy(w.at[rows], weights.at[k, rows], sems.at[PARTS * k + part])
            )
    fetch = []
    for k in range(N):
        fetch.append(
            pltpu.make_async_copy(
                x_hbm[k], xb.at[jnp.bitwise_xor(me_ref[0], k)], sems.at[5 * PARTS + k]
            )
        )
    for copy in copies[:PARTS] + fetch + copies[PARTS:]:
        copy.start()

    def weight(k):
        if k == 0:
            for copy in copies[:PARTS] + fetch:
                copy.wait()
        if k == 1:
            for copy in copies[PARTS:]:
                copy.wait()
        return weights[k]

    halves = []
    for pick in (lanes_lo, lanes_hi):
        halves.append(
            jnp.concatenate(
                [
                    pick(mr_ref[512 * t : 512 * t + 256, :], mr_ref[512 * t + 256 : 512 * t + 512, :])
                    for t in range(H // 2)
                ],
                axis=1,
            )
        )
    mixed = jnp.concatenate(halves, axis=0)
    ysc[...] = mm(mixed, weight(0)).reshape(2, N, 2, 8, E)
    xsc[...] = xb[...].astype(f32).reshape(N, 2, 2, 8, XW)
    blocks = []
    masks = []
    for i in range(2):
        for s2 in range(2):
            blocks.append((ysc[s2, :, i] + xsc[:, i, s2, :, :E]).reshape(128, E))
            masks.append(xsc[:, i, s2, :, E:].reshape(128, 128))
    after_rows = jnp.concatenate(blocks, axis=0).astype(bf16)
    wide = after_rows.astype(f32)
    mask = jnp.concatenate(masks, axis=0).astype(bf16)
    lane0 = jnp.where(
        lax.broadcasted_iota(jnp.int32, (8, 128), 1) == 0, 1.0, 0.0
    ).astype(bf16)
    alive = mmt(lane0, mask)

    normed = norm(wide)
    qs[...] = mm(normed, weight(1)).astype(bf16)
    ks[...] = mm(normed, weight(2)).astype(bf16)
    vs[...] = mm(normed, weight(3)).astype(bf16)
    low = lax.broadcasted_iota(jnp.int32, (SEQS, 128), 1) < 64
    for i in range(2):
        rows = slice(SEQS * i, SEQS * i + SEQS)
        keep = alive[0:1, rows] > 0
        for t in range(H // 2):
            lanes = slice(128 * t, 128 * t + 128)
            q, k, v = qs[rows, lanes], ks[rows, lanes], vs[rows, lanes]
            mixes = []
            for own in (low, jnp.logical_not(low)):
                logits = mmt(jnp.where(own, q, jnp.zeros_like(q)), k) * 0.125
                logits = jnp.where(keep, logits, -1000000000.0)
                e = jnp.exp(logits - jnp.max(logits, axis=-1, keepdims=True))
                p = (e * (1.0 / jnp.sum(e, axis=-1, keepdims=True))).astype(bf16)
                mixes.append(mm(p, v))
            ms[rows, lanes] = jnp.where(low, mixes[0], mixes[1]).astype(bf16)

    out = (wide + mm(ms[...], weight(4))).astype(bf16)
    out_wide = out.astype(f32)
    for i in range(2):
        for s2 in range(2):
            at = SEQS * i + 128 * s2
            xsc[:, i, s2, :, :E] = out_wide[at : at + 128].reshape(N, 8, E)
    out_ref[:, :I] = xsc[:, :, :, :, :E].reshape(N, I, E).astype(bf16)

    f = jnp.concatenate([f1_ref[...], f2_ref[...]], axis=0)
    factors = (mmt(f, norm(out_wide)) * alive[0:1, :]).astype(bf16)
    for i in range(2):
        r_ref[C * i : C * i + C, :] = factors[C:, SEQS * i : SEQS * i + SEQS]
    counts = [
        jnp.sum(alive[0:1, SEQS * i : SEQS * i + SEQS], axis=-1, keepdims=True)
        for i in range(2)
    ]
    row = lax.broadcasted_iota(jnp.int32, (C, SEQS), 0)
    count = jnp.where(row == 0, counts[0], counts[1]).astype(bf16)
    r_ref[2 * C :, :] = count[: RW - 2 * C, :]
    left = jnp.concatenate([factors[:C, :], count], axis=1)
    for k in range(N):
        out_ref[k, I:] = left


def column_step(me, mr, f1, f2, wo, cq, ck, cv, co, xs):
    return pl.pallas_call(
        column_kernel,
        in_specs=[pl.BlockSpec(memory_space=pltpu.SMEM)] + whole(3) + [HBM] * (5 + N),
        out_specs=whole(2),
        out_shape=[
            jax.ShapeDtypeStruct((N, 2 * I, E), bf16),
            jax.ShapeDtypeStruct((RW, SEQS), bf16),
        ],
        scratch_shapes=[
            pltpu.VMEM((2, N, 2, 8, E), f32),
            pltpu.VMEM((N, 2, 2, 8, XW), f32),
            pltpu.VMEM((ROWS, E), bf16),
            pltpu.VMEM((ROWS, E), bf16),
            pltpu.VMEM((ROWS, E), bf16),
            pltpu.VMEM((ROWS, E), bf16),
            pltpu.VMEM((5, E, E), bf16),
            pltpu.VMEM((N, I, XW), bf16),
            pltpu.SemaphoreType.DMA((5 * PARTS + N,)),
        ],
        compiler_params=params(59),
        cost_estimate=cost(5 * 2 * ROWS * E * E, 9_000_000, 2 * H * SEQS * SEQS),
    )(me, mr, f1, f2, wo, cq, ck, cv, co, *xs)


def back_kernel(in_ref, out_ref):
    o = lax.broadcasted_iota(jnp.int32, (ROWS, ROWS), 0)
    r = lax.broadcasted_iota(jnp.int32, (ROWS, ROWS), 1)
    src = (((o >> 1) & 15) << 5) + ((o & 1) << 4) + (o >> 5)
    perm = jnp.where(src == r, 1.0, 0.0).astype(bf16)
    out_ref[...] = mm(perm, in_ref[...].reshape(ROWS, E)).astype(bf16)


def back(both):
    return pl.pallas_call(
        back_kernel,
        grid=(1,),
        in_specs=[pl.BlockSpec((N, I, E), lambda n: (0, 0, 0))],
        out_specs=pl.BlockSpec((ROWS, E), lambda n: (0, 0)),
        out_shape=jax.ShapeDtypeStruct((ROWS, E), bf16),
        compiler_params=params(24),
        cost_estimate=cost(2 * ROWS * ROWS * E, 2_000_000),
    )(both)


def pair_kernel(
    me_ref, l_ref, r0, r1, r2, r3, wp_ref, out_ref,
    l0, l1, l2, l3, l4, lp, lhs, osc, wk, r_ref, n_ref,
):
    for near, ref in enumerate((r0, r1, r2, r3)):
        for far in range(4):
            at = jnp.bitwise_xor(me_ref[1], 4 * far + near)
            r_ref[at] = ref[2 * C * far : 2 * C * far + 2 * C]
            n_ref[at] = ref[8 * C + 4 * far : 8 * C + 4 * far + 4, :128].astype(f32)
    wk[...] = jnp.zeros_like(wk)
    for c in range(C):
        w = wp_ref[C * c : C * c + C, :]
        for j in range(4):
            at = 128 * c + C * j
            wk[at : at + C, 128 * j : 128 * j + 128] = w
    every = l_ref[...].reshape(N * C, E).astype(f32)
    for k, ref in enumerate((l0, l1, l2, l3, l4)):
        ref[...] = every[:, 128 * k : 128 * k + 128]

    def across(ref, row):
        return ref[pl.ds(row, N, stride=C), :]

    for c in range(C):
        rows = slice(C * c, C * c + C)
        lp[rows, :128] = jnp.concatenate([across(l0, c), across(l2, c)], axis=0).astype(bf16)
        lp[rows, 128:] = jnp.concatenate([across(l1, c), across(l3, c)], axis=0).astype(bf16)
    left_count = jnp.concatenate([across(l4, 0), across(l4, 1)], axis=0)
    right = r_ref[...].reshape(N * 2 * C, SEQS)
    for c in range(0, C, 4):
        outer = mmt(lp[C * c : C * c + 4 * C, :], right).astype(bf16)
        for k in range(4):
            for j in range(8):
                lhs[C * j : C * j + C, 128 * (c + k) : 128 * (c + k) + 128] = outer[
                    C * k : C * k + C, 128 * j : 128 * j + 128
                ]
    acc = mm(lhs[...], wk[...])
    right_count = n_ref[...]
    for j in range(C):
        part = acc[C * (j // 4) : C * (j // 4) + C, 128 * (j % 4) : 128 * (j % 4) + 128]
        count = right_count[j // 2, j % 2 : j % 2 + 1, :]
        part = part / (jnp.minimum(left_count, count) + 0.001)
        for i in range(2):
            osc[pl.ds(C * i + j, N, stride=2 * C), :] = part[N * i : N * i + N, :]
    out_ref[...] = osc[...].astype(bf16)


def pair_step(me, both, rights, wp):
    return pl.pallas_call(
        pair_kernel,
        grid=(1,),
        in_specs=[
            pl.BlockSpec(memory_space=pltpu.SMEM),
            pl.BlockSpec((N, I, E), lambda n: (0, 1, 0)),
        ]
        + [pl.BlockSpec((8 * C + 16, SEQS), lambda n: (0, 0))] * 4
        + [pl.BlockSpec((C * C, PC), lambda n: (0, 0))],
        out_specs=pl.BlockSpec((C * C, PC), lambda n: (0, 0)),
        out_shape=jax.ShapeDtypeStruct((C * C, PC), bf16),
        scratch_shapes=[pltpu.VMEM((N * C, 128), f32)] * 5
        + [
            pltpu.VMEM((1024, SEQS), bf16),
            pltpu.VMEM((256, 4096), bf16),
            pltpu.VMEM((1024, PC), f32),
            pltpu.VMEM((4096, 512), bf16),
            pltpu.VMEM((N, 2 * C, SEQS), bf16),
            pltpu.VMEM((N, 4, 128), f32),
        ],
        compiler_params=params(24),
        cost_estimate=cost(2 * 1024 * 1024 * 256 + 2 * 256 * 4096 * 512, 6_000_000),
    )(me, both, *rights, wp)


def exchange(x, axis):
    return lax.all_to_all(x, axis, split_axis=0, concat_axis=0, tiled=True)


def swap(x):
    pairs = [(N * d + g, N * g + d) for d in range(N) for g in range(N)]
    return lax.ppermute(x, ("depth", "cols"), pairs)


def mirror(x, k, axis):
    return lax.ppermute(x, axis, [(d, d ^ k) for d in range(N)])


def on_device(x, occupancy, wq, wk, wv, wo, cq, ck, cv, co, f1, f2, wp):
    x = x.reshape(ROWS, E)

    me = jnp.stack([lax.axis_index("depth"), lax.axis_index("cols")]).astype(jnp.int32)

    sent = row_proj(x, occupancy, wq, wk, wv)
    qkv = exchange(sent, "cols")
    later, _ = lax.optimization_barrier((x, sent))
    xs = list(turn(me, later, occupancy))
    for k in range(1, N):
        xs[k] = mirror(xs[k], k, "depth")
    qkv, xs = lax.optimization_barrier((qkv, xs))

    parts = exchange(partial_logits(qkv).reshape(N, I, SITES), "depth")
    p = exchange(row_softmax(parts), "depth")
    mix = row_mix(p, qkv)
    mr = exchange(mix.reshape(N * N, 16, 128), ("cols", "depth")).reshape(4096, 128)

    both, right = column_step(me, mr, f1.T, f2.T, wo, cq, ck, cv, co, xs)
    both = exchange(both, "depth")
    right = swap(right)
    far = [right] + [mirror(right, 4 * k, "cols") for k in range(1, 4)]
    counts = [part[2 * C : 2 * C + 4] for part in far]
    far = jnp.concatenate([part[: 2 * C] for part in far] + counts, axis=0)
    rights = [far] + [mirror(far, k, "cols") for k in range(1, 4)]
    out = back(both)
    pair = pair_step(me, both, rights, wp)
    return out.reshape(S, I, E), pair.reshape(C, C, PC)


def solution(mesh):
    placed = (P("depth", "cols", None), P("depth", "cols")) + (P(),) * 11
    return jax.shard_map(
        on_device,
        mesh=mesh,
        in_specs=placed,
        out_specs=(P("depth", "cols", None), P("cols", "depth", None)),
        check_vma=False,
    )
```

```python
import functools
import math

import jax
import jax.numpy as jnp
from jax import lax
from jax.experimental import pallas as pl
from jax.experimental.pallas import tpu as pltpu
from jax.sharding import PartitionSpec as P

f32 = jnp.float32
bf16 = jnp.bfloat16

S = 16
I = 32
E = 768
H = 12
N = 16
ROWS = S * I
SEQS = 256
SITES = 512
C = 32
PC = 128
XW = E + 128
RW = 80
PARTS = 1

NT = (((1,), (1,)), ((), ()))


def norm(wide):
    center = wide - jnp.mean(wide, axis=-1, keepdims=True)
    spread = jnp.mean(center * center, axis=-1, keepdims=True)
    return (center * lax.rsqrt(spread + 1e-05)).astype(bf16)


def mm(a, b):
    return jnp.dot(a, b, preferred_element_type=f32)


def mmt(a, b):
    return lax.dot_general(a, b, NT, preferred_element_type=f32)


def lanes_lo(a, b):
    return jnp.concatenate([a[:, :64], b[:, :64]], axis=1)


def lanes_hi(a, b):
    return jnp.concatenate([a[:, 64:], b[:, 64:]], axis=1)


HBM = pl.BlockSpec(memory_space=pltpu.HBM)


def whole(n):
    return [pl.BlockSpec(memory_space=pltpu.VMEM)] * n


def params(mib):
    return pltpu.CompilerParams(vmem_limit_bytes=int(mib * 1024 * 1024))


def cost(flops, bytes_accessed, transcendentals=0):
    return pl.CostEstimate(
        flops=flops, bytes_accessed=bytes_accessed, transcendentals=transcendentals
    )


def mask_rows(occupancy, width):
    s = lax.broadcasted_iota(jnp.int32, (ROWS, S), 0) // I
    own = s == lax.broadcasted_iota(jnp.int32, (ROWS, S), 1)
    spread = mm(jnp.where(own, 1.0, 0.0).astype(bf16), occupancy.astype(f32).astype(bf16))
    i = lax.broadcasted_iota(jnp.int32, (ROWS, I), 0) % I
    own = i == lax.broadcasted_iota(jnp.int32, (ROWS, I), 1)
    column = jnp.sum(jnp.where(own, spread, 0.0), axis=-1, keepdims=True)
    return jnp.broadcast_to(column, (ROWS, width))


def row_proj_kernel(
    x_hbm, occ_hbm, wq_hbm, wk_hbm, wv_hbm, out_hbm,
    xv, occ, wv, xn_ref, out, sems,
):
    first = [pltpu.make_async_copy(occ_hbm, occ, sems.at[0])]
    for k in range(4):
        rows = pl.ds(128 * k, 128)
        first.append(pltpu.make_async_copy(x_hbm.at[rows], xv.at[rows], sems.at[1 + k]))
    for copy in first:
        copy.start()
    tiles = [
        pltpu.make_async_copy(w, wv.at[k], sems.at[5 + k])
        for k, w in enumerate((wq_hbm, wk_hbm, wv_hbm))
    ]
    for copy in tiles:
        copy.start()
    first[0].wait()
    live = mask_rows(occ[...], 128)
    for k in range(4):
        first[1 + k].wait()
        rows = slice(128 * k, 128 * k + 128)
        xn_ref[rows] = norm(xv[rows].astype(f32))
    sent = []
    xn = xn_ref[...]
    half = ROWS // 2
    for copy in tiles:
        copy.wait()
    for index in range(3):
        rows = slice(256 * index, 256 * index + 256)
        for n in range(3):
            y = mm(xn, wv[index, :, 256 * n : 256 * n + 256])
            for t in range(2):
                part = y[:, 128 * t : 128 * t + 128]
                if index < 2:
                    part = part * live
                part = part.astype(bf16)
                a, b = part[:half], part[half:]
                out[4 * n + 2 * t, rows] = lanes_lo(a, b)
                out[4 * n + 2 * t + 1, rows] = lanes_hi(a, b)
        at = pl.ds(256 * index, 256)
        sent.append(
            pltpu.make_async_copy(
                out.at[:, at], out_hbm.at[pl.ds(0, H), at], sems.at[9 + index]
            )
        )
        sent[-1].start()
    for copy in sent:
        copy.wait()


def row_proj(x, occupancy, wq, wk, wv):
    return pl.pallas_call(
        row_proj_kernel,
        in_specs=[HBM] * 5,
        out_specs=HBM,
        out_shape=jax.ShapeDtypeStruct((N, 768, 128), bf16),
        scratch_shapes=[
            pltpu.VMEM((ROWS, E), bf16),
            pltpu.VMEM((S, I), jnp.int32),
            pltpu.VMEM((3, E, E), bf16),
            pltpu.VMEM((ROWS, E), bf16),
            pltpu.VMEM((H, 768, 128), bf16),
            pltpu.SemaphoreType.DMA((12,)),
        ],
        compiler_params=params(61),
        cost_estimate=cost(3 * 2 * ROWS * E * E, 8_000_000),
    )(x, occupancy, wq, wk, wv)


def turn_kernel(me_ref, x_ref, occ_ref, *out_refs):
    r = lax.broadcasted_iota(jnp.int32, (ROWS, ROWS), 0)
    o = lax.broadcasted_iota(jnp.int32, (ROWS, ROWS), 1)
    d = jnp.bitwise_xor(r >> 5, me_ref[0])
    src = ((r & 15) << 5) + (d << 1) + ((r >> 4) & 1)
    perm = jnp.where(src == o, 1.0, 0.0).astype(bf16)
    x = mm(perm, x_ref[...]).astype(bf16)
    mask = mm(perm, mask_rows(occ_ref[...], 128).astype(bf16)).astype(bf16)
    for k in range(N):
        out_refs[k][:, :E] = x[I * k : I * k + I]
        out_refs[k][:, E:] = mask[I * k : I * k + I]


def turn(me, x, occupancy):
    return pl.pallas_call(
        turn_kernel,
        in_specs=[pl.BlockSpec(memory_space=pltpu.SMEM)] + whole(2),
        out_specs=whole(N),
        out_shape=[jax.ShapeDtypeStruct((I, XW), bf16)] * N,
        compiler_params=params(16),
        cost_estimate=cost(2 * ROWS * ROWS * E, 3_000_000),
    )(me, x, occupancy)


def logits_kernel(qk_ref, out_ref):
    def side(k):
        return jnp.concatenate(
            [
                qk_ref[:, 256 * k + I * s : 256 * k + I * s + I, :].reshape(SITES, 128)
                for s in range(S // 2)
            ],
            axis=1,
        )

    out_ref[...] = (mmt(side(0), side(1)) * (1.0 / math.sqrt(64 * SEQS))).astype(bf16)


def partial_logits(qkv):
    return pl.pallas_call(
        logits_kernel,
        grid=(1,),
        in_specs=[pl.BlockSpec((N, 512, 128), lambda n: (0, 0, 0))],
        out_specs=pl.BlockSpec((SITES, SITES), lambda n: (0, 0)),
        out_shape=jax.ShapeDtypeStruct((SITES, SITES), bf16),
        compiler_params=params(20),
        cost_estimate=cost(2 * SITES * SITES * 1024, 3_000_000),
    )(qkv)


def softmax_kernel(in_ref, out_ref):
    total = in_ref[0].astype(f32)
    for k in range(1, N):
        total = total + in_ref[k].astype(f32)
    top = jnp.max(total, axis=-1, keepdims=True)
    e = jnp.exp(total - top)
    p = (e / jnp.sum(e, axis=-1, keepdims=True)).astype(bf16)
    for k in range(N):
        out_ref[k] = p


def row_softmax(parts):
    return pl.pallas_call(
        softmax_kernel,
        in_specs=whole(1),
        out_specs=pl.BlockSpec(memory_space=pltpu.VMEM),
        out_shape=jax.ShapeDtypeStruct((N, I, SITES), bf16),
        compiler_params=params(16),
        cost_estimate=cost(N * I * SITES, 4_000_000, I * SITES),
    )(parts)


def row_mix_kernel(p_ref, v_ref, out_ref):
    v = jnp.concatenate(
        [v_ref[:, I * s : I * s + I, :].reshape(SITES, 128) for s in range(S // 2)],
        axis=1,
    )
    mix = mm(p_ref[...].reshape(SITES, SITES), v).astype(bf16)
    r = lax.broadcasted_iota(jnp.int32, (256, 256), 0)
    o = lax.broadcasted_iota(jnp.int32, (256, 256), 1)
    perm = jnp.where(((r & 7) << 5) + (r >> 3) == o, 1.0, 0.0).astype(bf16)

    def block(b):
        part = mix[I * b : I * b + I, :]
        return jnp.concatenate(
            [part[:, 128 * s : 128 * s + 128] for s in range(8)], axis=0
        )

    for b in range(0, N, 2):
        pair = jnp.concatenate([block(b), block(b + 1)], axis=1)
        turned = mm(perm, pair).astype(bf16)
        out_ref[256 * b : 256 * b + 256, :] = turned[:, :128]
        out_ref[256 * b + 256 : 256 * b + 512, :] = turned[:, 128:]


def row_mix(p, qkv):
    return pl.pallas_call(
        row_mix_kernel,
        grid=(1,),
        in_specs=[
            pl.BlockSpec((N, I, SITES), lambda n: (0, 0, 0)),
            pl.BlockSpec((N, 256, 128), lambda n: (0, 2, 0)),
        ],
        out_specs=pl.BlockSpec((4096, 128), lambda n: (0, 0)),
        out_shape=jax.ShapeDtypeStruct((4096, 128), bf16),
        compiler_params=params(20),
        cost_estimate=cost(2 * SITES * SITES * 1024, 3_000_000),
    )(p, qkv)


def column_kernel(
    me_ref, mr_ref, f1_ref, f2_ref, wo_hbm, cq_hbm, ck_hbm, cv_hbm, co_hbm, *refs
):
    x_hbm, refs = refs[:N], refs[N:]
    out_ref, r_ref, ysc, xsc, qs, ks, vs, ms, weights, xb, sems = refs
    copies = []
    for k, w in enumerate((wo_hbm, cq_hbm, ck_hbm, cv_hbm, co_hbm)):
        for part in range(PARTS):
            rows = pl.ds(E // PARTS * part, E // PARTS)
            copies.append(
                pltpu.make_async_copy(w.at[rows], weights.at[k, rows], sems.at[PARTS * k + part])
            )
    fetch = []
    for k in range(N):
        fetch.append(
            pltpu.make_async_copy(
                x_hbm[k], xb.at[jnp.bitwise_xor(me_ref[0], k)], sems.at[5 * PARTS + k]
            )
        )
    for copy in copies[:PARTS] + fetch + copies[PARTS:]:
        copy.start()

    def weight(k):
        if k == 0:
            for copy in copies[:PARTS] + fetch:
                copy.wait()
        if k == 1:
            for copy in copies[PARTS:]:
                copy.wait()
        return weights[k]

    halves = []
    for pick in (lanes_lo, lanes_hi):
        halves.append(
            jnp.concatenate(
                [
                    pick(mr_ref[512 * t : 512 * t + 256, :], mr_ref[512 * t + 256 : 512 * t + 512, :])
                    for t in range(H // 2)
                ],
                axis=1,
            )
        )
    mixed = jnp.concatenate(halves, axis=0)
    ysc[...] = mm(mixed, weight(0)).reshape(2, N, 2, 8, E)
    xsc[...] = xb[...].astype(f32).reshape(N, 2, 2, 8, XW)
    blocks = []
    masks = []
    for i in range(2):
        for s2 in range(2):
            blocks.append((ysc[s2, :, i] + xsc[:, i, s2, :, :E]).reshape(128, E))
            masks.append(xsc[:, i, s2, :, E:].reshape(128, 128))
    after_rows = jnp.concatenate(blocks, axis=0).astype(bf16)
    wide = after_rows.astype(f32)
    mask = jnp.concatenate(masks, axis=0).astype(bf16)
    lane0 = jnp.where(
        lax.broadcasted_iota(jnp.int32, (8, 128), 1) == 0, 1.0, 0.0
    ).astype(bf16)
    alive = mmt(lane0, mask)

    normed = norm(wide)
    qs[...] = mm(normed, weight(1)).astype(bf16)
    ks[...] = mm(normed, weight(2)).astype(bf16)
    vs[...] = mm(normed, weight(3)).astype(bf16)
    low = lax.broadcasted_iota(jnp.int32, (SEQS, 128), 1) < 64
    for i in range(2):
        rows = slice(SEQS * i, SEQS * i + SEQS)
        keep = alive[0:1, rows] > 0
        for t in range(H // 2):
            lanes = slice(128 * t, 128 * t + 128)
            q, k, v = qs[rows, lanes], ks[rows, lanes], vs[rows, lanes]
            mixes = []
            for own in (low, jnp.logical_not(low)):
                logits = mmt(jnp.where(own, q, jnp.zeros_like(q)), k) * 0.125
                logits = jnp.where(keep, logits, -1000000000.0)
                e = jnp.exp(logits - jnp.max(logits, axis=-1, keepdims=True))
                total = jnp.sum(e, axis=-1, keepdims=True)
                mixes.append(mm(e.astype(bf16), v) * (1.0 / total))
            ms[rows, lanes] = jnp.where(low, mixes[0], mixes[1]).astype(bf16)

    out = (wide + mm(ms[...], weight(4))).astype(bf16)
    out_wide = out.astype(f32)
    for i in range(2):
        for s2 in range(2):
            at = SEQS * i + 128 * s2
            xsc[:, i, s2, :, :E] = out_wide[at : at + 128].reshape(N, 8, E)
    out_ref[:, :I] = xsc[:, :, :, :, :E].reshape(N, I, E).astype(bf16)

    f = jnp.concatenate([f1_ref[...], f2_ref[...]], axis=0)
    factors = (mmt(f, norm(out_wide)) * alive[0:1, :]).astype(bf16)
    for i in range(2):
        r_ref[C * i : C * i + C, :] = factors[C:, SEQS * i : SEQS * i + SEQS]
    counts = [
        jnp.sum(alive[0:1, SEQS * i : SEQS * i + SEQS], axis=-1, keepdims=True)
        for i in range(2)
    ]
    row = lax.broadcasted_iota(jnp.int32, (C, SEQS), 0)
    count = jnp.where(row == 0, counts[0], counts[1]).astype(bf16)
    r_ref[2 * C :, :] = count[: RW - 2 * C, :]
    left = jnp.concatenate([factors[:C, :], count], axis=1)
    for k in range(N):
        out_ref[k, I:] = left


def column_step(me, mr, f1, f2, wo, cq, ck, cv, co, xs):
    return pl.pallas_call(
        column_kernel,
        in_specs=[pl.BlockSpec(memory_space=pltpu.SMEM)] + whole(3) + [HBM] * (5 + N),
        out_specs=whole(2),
        out_shape=[
            jax.ShapeDtypeStruct((N, 2 * I, E), bf16),
            jax.ShapeDtypeStruct((RW, SEQS), bf16),
        ],
        scratch_shapes=[
            pltpu.VMEM((2, N, 2, 8, E), f32),
            pltpu.VMEM((N, 2, 2, 8, XW), f32),
            pltpu.VMEM((ROWS, E), bf16),
            pltpu.VMEM((ROWS, E), bf16),
            pltpu.VMEM((ROWS, E), bf16),
            pltpu.VMEM((ROWS, E), bf16),
            pltpu.VMEM((5, E, E), bf16),
            pltpu.VMEM((N, I, XW), bf16),
            pltpu.SemaphoreType.DMA((5 * PARTS + N,)),
        ],
        compiler_params=params(59),
        cost_estimate=cost(5 * 2 * ROWS * E * E, 9_000_000, 2 * H * SEQS * SEQS),
    )(me, mr, f1, f2, wo, cq, ck, cv, co, *xs)


def back_kernel(in_ref, out_ref):
    o = lax.broadcasted_iota(jnp.int32, (ROWS, ROWS), 0)
    r = lax.broadcasted_iota(jnp.int32, (ROWS, ROWS), 1)
    src = (((o >> 1) & 15) << 5) + ((o & 1) << 4) + (o >> 5)
    perm = jnp.where(src == r, 1.0, 0.0).astype(bf16)
    out_ref[...] = mm(perm, in_ref[...].reshape(ROWS, E)).astype(bf16)


def back(both):
    return pl.pallas_call(
        back_kernel,
        grid=(1,),
        in_specs=[pl.BlockSpec((N, I, E), lambda n: (0, 0, 0))],
        out_specs=pl.BlockSpec((ROWS, E), lambda n: (0, 0)),
        out_shape=jax.ShapeDtypeStruct((ROWS, E), bf16),
        compiler_params=params(24),
        cost_estimate=cost(2 * ROWS * ROWS * E, 2_000_000),
    )(both)


def pair_kernel(
    me_ref, l_ref, r0, r1, r2, r3, wp_ref, out_ref,
    l0, l1, l2, l3, l4, lp, lhs, osc, wk, r_ref, n_ref,
):
    for near, ref in enumerate((r0, r1, r2, r3)):
        for far in range(4):
            at = jnp.bitwise_xor(me_ref[1], 4 * far + near)
            r_ref[at] = ref[2 * C * far : 2 * C * far + 2 * C]
            n_ref[at] = ref[8 * C + 4 * far : 8 * C + 4 * far + 4, :128].astype(f32)
    wk[...] = jnp.zeros_like(wk)
    for c in range(C):
        w = wp_ref[C * c : C * c + C, :]
        for j in range(4):
            at = 128 * c + C * j
            wk[at : at + C, 128 * j : 128 * j + 128] = w
    every = l_ref[...].reshape(N * C, E).astype(f32)
    for k, ref in enumerate((l0, l1, l2, l3, l4)):
        ref[...] = every[:, 128 * k : 128 * k + 128]

    def across(ref, row):
        return ref[pl.ds(row, N, stride=C), :]

    for c in range(C):
        rows = slice(C * c, C * c + C)
        lp[rows, :128] = jnp.concatenate([across(l0, c), across(l2, c)], axis=0).astype(bf16)
        lp[rows, 128:] = jnp.concatenate([across(l1, c), across(l3, c)], axis=0).astype(bf16)
    left_count = jnp.concatenate([across(l4, 0), across(l4, 1)], axis=0)
    right = r_ref[...].reshape(N * 2 * C, SEQS)
    for c in range(0, C, 4):
        outer = mmt(lp[C * c : C * c + 4 * C, :], right).astype(bf16)
        for k in range(4):
            for j in range(8):
                lhs[C * j : C * j + C, 128 * (c + k) : 128 * (c + k) + 128] = outer[
                    C * k : C * k + C, 128 * j : 128 * j + 128
                ]
    acc = mm(lhs[...], wk[...])
    right_count = n_ref[...]
    for j in range(C):
        part = acc[C * (j // 4) : C * (j // 4) + C, 128 * (j % 4) : 128 * (j % 4) + 128]
        count = right_count[j // 2, j % 2 : j % 2 + 1, :]
        part = part / (jnp.minimum(left_count, count) + 0.001)
        for i in range(2):
            osc[pl.ds(C * i + j, N, stride=2 * C), :] = part[N * i : N * i + N, :]
    out_ref[...] = osc[...].astype(bf16)


def pair_step(me, both, rights, wp):
    return pl.pallas_call(
        pair_kernel,
        grid=(1,),
        in_specs=[
            pl.BlockSpec(memory_space=pltpu.SMEM),
            pl.BlockSpec((N, I, E), lambda n: (0, 1, 0)),
        ]
        + [pl.BlockSpec((8 * C + 16, SEQS), lambda n: (0, 0))] * 4
        + [pl.BlockSpec((C * C, PC), lambda n: (0, 0))],
        out_specs=pl.BlockSpec((C * C, PC), lambda n: (0, 0)),
        out_shape=jax.ShapeDtypeStruct((C * C, PC), bf16),
        scratch_shapes=[pltpu.VMEM((N * C, 128), f32)] * 5
        + [
            pltpu.VMEM((1024, SEQS), bf16),
            pltpu.VMEM((256, 4096), bf16),
            pltpu.VMEM((1024, PC), f32),
            pltpu.VMEM((4096, 512), bf16),
            pltpu.VMEM((N, 2 * C, SEQS), bf16),
            pltpu.VMEM((N, 4, 128), f32),
        ],
        compiler_params=params(24),
        cost_estimate=cost(2 * 1024 * 1024 * 256 + 2 * 256 * 4096 * 512, 6_000_000),
    )(me, both, *rights, wp)


def exchange(x, axis):
    return lax.all_to_all(x, axis, split_axis=0, concat_axis=0, tiled=True)


def swap(x):
    pairs = [(N * d + g, N * g + d) for d in range(N) for g in range(N)]
    return lax.ppermute(x, ("depth", "cols"), pairs)


def mirror(x, k, axis):
    return lax.ppermute(x, axis, [(d, d ^ k) for d in range(N)])


def on_device(x, occupancy, wq, wk, wv, wo, cq, ck, cv, co, f1, f2, wp):
    x = x.reshape(ROWS, E)

    me = jnp.stack([lax.axis_index("depth"), lax.axis_index("cols")]).astype(jnp.int32)

    sent = row_proj(x, occupancy, wq, wk, wv)
    qkv = exchange(sent, "cols")
    later, _ = lax.optimization_barrier((x, sent))
    xs = list(turn(me, later, occupancy))
    for k in range(1, N):
        xs[k] = mirror(xs[k], k, "depth")
    qkv, xs = lax.optimization_barrier((qkv, xs))

    parts = exchange(partial_logits(qkv).reshape(N, I, SITES), "depth")
    p = exchange(row_softmax(parts), "depth")
    mix = row_mix(p, qkv)
    mr = exchange(mix.reshape(N * N, 16, 128), ("cols", "depth")).reshape(4096, 128)

    both, right = column_step(me, mr, f1.T, f2.T, wo, cq, ck, cv, co, xs)
    both = exchange(both, "depth")
    right = swap(right)
    far = [right] + [mirror(right, 4 * k, "cols") for k in range(1, 4)]
    counts = [part[2 * C : 2 * C + 4] for part in far]
    far = jnp.concatenate([part[: 2 * C] for part in far] + counts, axis=0)
    rights = [far] + [mirror(far, k, "cols") for k in range(1, 4)]
    out = back(both)
    pair = pair_step(me, both, rights, wp)
    return out.reshape(S, I, E), pair.reshape(C, C, PC)


def solution(mesh):
    placed = (P("depth", "cols", None), P("depth", "cols")) + (P(),) * 11
    return jax.shard_map(
        on_device,
        mesh=mesh,
        in_specs=placed,
        out_specs=(P("depth", "cols", None), P("cols", "depth", None)),
        check_vma=False,
    )
```

```python
import functools
import math

import jax
import jax.numpy as jnp
from jax import lax
from jax.experimental import pallas as pl
from jax.experimental.pallas import tpu as pltpu
from jax.sharding import PartitionSpec as P

f32 = jnp.float32
bf16 = jnp.bfloat16

S = 16
I = 32
E = 768
H = 12
N = 16
ROWS = S * I
SEQS = 256
SITES = 512
C = 32
PC = 128
XW = E + 128
RW = 80
PARTS = 1

NT = (((1,), (1,)), ((), ()))


def norm(wide):
    center = wide - jnp.mean(wide, axis=-1, keepdims=True)
    spread = jnp.mean(center * center, axis=-1, keepdims=True)
    return (center * lax.rsqrt(spread + 1e-05)).astype(bf16)


def mm(a, b):
    return jnp.dot(a, b, preferred_element_type=f32)


def mmt(a, b):
    return lax.dot_general(a, b, NT, preferred_element_type=f32)


def lanes_lo(a, b):
    return jnp.concatenate([a[:, :64], b[:, :64]], axis=1)


def lanes_hi(a, b):
    return jnp.concatenate([a[:, 64:], b[:, 64:]], axis=1)


HBM = pl.BlockSpec(memory_space=pltpu.HBM)


def whole(n):
    return [pl.BlockSpec(memory_space=pltpu.VMEM)] * n


def params(mib):
    return pltpu.CompilerParams(vmem_limit_bytes=int(mib * 1024 * 1024))


def cost(flops, bytes_accessed, transcendentals=0):
    return pl.CostEstimate(
        flops=flops, bytes_accessed=bytes_accessed, transcendentals=transcendentals
    )


def mask_rows(occupancy, width):
    s = lax.broadcasted_iota(jnp.int32, (ROWS, S), 0) // I
    own = s == lax.broadcasted_iota(jnp.int32, (ROWS, S), 1)
    spread = mm(jnp.where(own, 1.0, 0.0).astype(bf16), occupancy.astype(f32).astype(bf16))
    i = lax.broadcasted_iota(jnp.int32, (ROWS, I), 0) % I
    own = i == lax.broadcasted_iota(jnp.int32, (ROWS, I), 1)
    column = jnp.sum(jnp.where(own, spread, 0.0), axis=-1, keepdims=True)
    return jnp.broadcast_to(column, (ROWS, width))


def row_proj_kernel(
    x_hbm, occ_hbm, wq_hbm, wk_hbm, wv_hbm, out_hbm,
    xv, occ, wv, xn_ref, out, sems,
):
    first = [pltpu.make_async_copy(occ_hbm, occ, sems.at[0])]
    for k in range(4):
        rows = pl.ds(128 * k, 128)
        first.append(pltpu.make_async_copy(x_hbm.at[rows], xv.at[rows], sems.at[1 + k]))
    for copy in first:
        copy.start()
    tiles = [
        pltpu.make_async_copy(w, wv.at[k], sems.at[5 + k])
        for k, w in enumerate((wq_hbm, wk_hbm, wv_hbm))
    ]
    for copy in tiles:
        copy.start()
    first[0].wait()
    live = mask_rows(occ[...], 128)
    for k in range(4):
        first[1 + k].wait()
        rows = slice(128 * k, 128 * k + 128)
        xn_ref[rows] = norm(xv[rows].astype(f32))
    sent = []
    xn = xn_ref[...]
    half = ROWS // 2
    for copy in tiles:
        copy.wait()
    for index in range(3):
        rows = slice(256 * index, 256 * index + 256)
        for n in range(3):
            y = mm(xn, wv[index, :, 256 * n : 256 * n + 256])
            for t in range(2):
                part = y[:, 128 * t : 128 * t + 128]
                if index < 2:
                    part = part * live
                part = part.astype(bf16)
                a, b = part[:half], part[half:]
                out[4 * n + 2 * t, rows] = lanes_lo(a, b)
                out[4 * n + 2 * t + 1, rows] = lanes_hi(a, b)
        at = pl.ds(256 * index, 256)
        sent.append(
            pltpu.make_async_copy(
                out.at[:, at], out_hbm.at[pl.ds(0, H), at], sems.at[9 + index]
            )
        )
        sent[-1].start()
    for copy in sent:
        copy.wait()


def row_proj(x, occupancy, wq, wk, wv):
    return pl.pallas_call(
        row_proj_kernel,
        in_specs=[HBM] * 5,
        out_specs=HBM,
        out_shape=jax.ShapeDtypeStruct((N, 768, 128), bf16),
        scratch_shapes=[
            pltpu.VMEM((ROWS, E), bf16),
            pltpu.VMEM((S, I), jnp.int32),
            pltpu.VMEM((3, E, E), bf16),
            pltpu.VMEM((ROWS, E), bf16),
            pltpu.VMEM((H, 768, 128), bf16),
            pltpu.SemaphoreType.DMA((12,)),
        ],
        compiler_params=params(61),
        cost_estimate=cost(3 * 2 * ROWS * E * E, 8_000_000),
    )(x, occupancy, wq, wk, wv)


def turn_kernel(me_ref, x_ref, occ_ref, *out_refs):
    r = lax.broadcasted_iota(jnp.int32, (ROWS, ROWS), 0)
    o = lax.broadcasted_iota(jnp.int32, (ROWS, ROWS), 1)
    d = jnp.bitwise_xor(r >> 5, me_ref[0])
    src = ((r & 15) << 5) + (d << 1) + ((r >> 4) & 1)
    perm = jnp.where(src == o, 1.0, 0.0).astype(bf16)
    x = mm(perm, x_ref[...]).astype(bf16)
    mask = mm(perm, mask_rows(occ_ref[...], 128).astype(bf16)).astype(bf16)
    for k in range(N):
        out_refs[k][:, :E] = x[I * k : I * k + I]
        out_refs[k][:, E:] = mask[I * k : I * k + I]


def turn(me, x, occupancy):
    return pl.pallas_call(
        turn_kernel,
        in_specs=[pl.BlockSpec(memory_space=pltpu.SMEM)] + whole(2),
        out_specs=whole(N),
        out_shape=[jax.ShapeDtypeStruct((I, XW), bf16)] * N,
        compiler_params=params(16),
        cost_estimate=cost(2 * ROWS * ROWS * E, 3_000_000),
    )(me, x, occupancy)


def logits_kernel(qk_ref, out_ref):
    def side(k):
        return jnp.concatenate(
            [
                qk_ref[:, 256 * k + I * s : 256 * k + I * s + I, :].reshape(SITES, 128)
                for s in range(S // 2)
            ],
            axis=1,
        )

    out_ref[...] = (mmt(side(0), side(1)) * (1.0 / math.sqrt(64 * SEQS))).astype(bf16)


def partial_logits(qkv):
    return pl.pallas_call(
        logits_kernel,
        grid=(1,),
        in_specs=[pl.BlockSpec((N, 512, 128), lambda n: (0, 0, 0))],
        out_specs=pl.BlockSpec((SITES, SITES), lambda n: (0, 0)),
        out_shape=jax.ShapeDtypeStruct((SITES, SITES), bf16),
        compiler_params=params(20),
        cost_estimate=cost(2 * SITES * SITES * 1024, 3_000_000),
    )(qkv)


def softmax_kernel(in_ref, out_ref):
    total = in_ref[0].astype(f32)
    for k in range(1, N):
        total = total + in_ref[k].astype(f32)
    top = jnp.max(total, axis=-1, keepdims=True)
    e = jnp.exp(total - top)
    p = (e / jnp.sum(e, axis=-1, keepdims=True)).astype(bf16)
    for k in range(N):
        out_ref[k] = p


def row_softmax(parts):
    return pl.pallas_call(
        softmax_kernel,
        in_specs=whole(1),
        out_specs=pl.BlockSpec(memory_space=pltpu.VMEM),
        out_shape=jax.ShapeDtypeStruct((N, I, SITES), bf16),
        compiler_params=params(16),
        cost_estimate=cost(N * I * SITES, 4_000_000, I * SITES),
    )(parts)


def row_mix_kernel(p_ref, v_ref, out_ref):
    v = jnp.concatenate(
        [v_ref[:, I * s : I * s + I, :].reshape(SITES, 128) for s in range(S // 2)],
        axis=1,
    )
    mix = mm(p_ref[...].reshape(SITES, SITES), v).astype(bf16)
    r = lax.broadcasted_iota(jnp.int32, (256, 256), 0)
    o = lax.broadcasted_iota(jnp.int32, (256, 256), 1)
    perm = jnp.where(((r & 7) << 5) + (r >> 3) == o, 1.0, 0.0).astype(bf16)

    def block(b):
        part = mix[I * b : I * b + I, :]
        return jnp.concatenate(
            [part[:, 128 * s : 128 * s + 128] for s in range(8)], axis=0
        )

    for b in range(0, N, 2):
        pair = jnp.concatenate([block(b), block(b + 1)], axis=1)
        turned = mm(perm, pair).astype(bf16)
        out_ref[256 * b : 256 * b + 256, :] = turned[:, :128]
        out_ref[256 * b + 256 : 256 * b + 512, :] = turned[:, 128:]


def row_mix(p, qkv):
    return pl.pallas_call(
        row_mix_kernel,
        grid=(1,),
        in_specs=[
            pl.BlockSpec((N, I, SITES), lambda n: (0, 0, 0)),
            pl.BlockSpec((N, 256, 128), lambda n: (0, 2, 0)),
        ],
        out_specs=pl.BlockSpec((4096, 128), lambda n: (0, 0)),
        out_shape=jax.ShapeDtypeStruct((4096, 128), bf16),
        compiler_params=params(20),
        cost_estimate=cost(2 * SITES * SITES * 1024, 3_000_000),
    )(p, qkv)


def column_kernel(
    me_ref, mr_ref, f1_ref, f2_ref, wo_hbm, cq_hbm, ck_hbm, cv_hbm, co_hbm, *refs
):
    x_hbm, refs = refs[:N], refs[N:]
    out_ref, r_ref, ysc, xsc, qs, ks, vs, ms, weights, xb, sems = refs
    copies = []
    for k, w in enumerate((wo_hbm, cq_hbm, ck_hbm, cv_hbm, co_hbm)):
        for part in range(PARTS):
            rows = pl.ds(E // PARTS * part, E // PARTS)
            copies.append(
                pltpu.make_async_copy(w.at[rows], weights.at[k, rows], sems.at[PARTS * k + part])
            )
    fetch = []
    for k in range(N):
        fetch.append(
            pltpu.make_async_copy(
                x_hbm[k], xb.at[jnp.bitwise_xor(me_ref[0], k)], sems.at[5 * PARTS + k]
            )
        )
    for copy in copies[:PARTS] + fetch + copies[PARTS:]:
        copy.start()

    def weight(k):
        if k == 0:
            for copy in copies[:PARTS] + fetch:
                copy.wait()
        if k == 1:
            for copy in copies[PARTS:]:
                copy.wait()
        return weights[k]

    halves = []
    for pick in (lanes_lo, lanes_hi):
        halves.append(
            jnp.concatenate(
                [
                    pick(mr_ref[512 * t : 512 * t + 256, :], mr_ref[512 * t + 256 : 512 * t + 512, :])
                    for t in range(H // 2)
                ],
                axis=1,
            )
        )
    mixed = jnp.concatenate(halves, axis=0)
    ysc[...] = mm(mixed, weight(0)).reshape(2, N, 2, 8, E)
    xsc[...] = xb[...].astype(f32).reshape(N, 2, 2, 8, XW)
    blocks = []
    masks = []
    for i in range(2):
        for s2 in range(2):
            blocks.append((ysc[s2, :, i] + xsc[:, i, s2, :, :E]).reshape(128, E))
            masks.append(xsc[:, i, s2, :, E:].reshape(128, 128))
    after_rows = jnp.concatenate(blocks, axis=0).astype(bf16)
    wide = after_rows.astype(f32)
    mask = jnp.concatenate(masks, axis=0).astype(bf16)
    lane0 = jnp.where(
        lax.broadcasted_iota(jnp.int32, (8, 128), 1) == 0, 1.0, 0.0
    ).astype(bf16)
    alive = mmt(lane0, mask)

    normed = norm(wide)
    qs[...] = mm(normed, weight(1)).astype(bf16)
    ks[...] = mm(normed, weight(2)).astype(bf16)
    vs[...] = mm(normed, weight(3)).astype(bf16)
    low = lax.broadcasted_iota(jnp.int32, (SEQS, 128), 1) < 64
    for i in range(2):
        rows = slice(SEQS * i, SEQS * i + SEQS)
        keep = alive[0:1, rows] > 0
        for t in range(H // 2):
            lanes = slice(128 * t, 128 * t + 128)
            q, k, v = qs[rows, lanes], ks[rows, lanes], vs[rows, lanes]
            mixes = []
            for own in (low, jnp.logical_not(low)):
                logits = mmt(jnp.where(own, q, jnp.zeros_like(q)), k) * 0.125
                logits = jnp.where(keep, logits, -1000000000.0)
                e = jnp.exp(logits - jnp.max(logits, axis=-1, keepdims=True))
                total = jnp.sum(e, axis=-1, keepdims=True)
                mixes.append(mm(e.astype(bf16), v) * (1.0 / total))
            ms[rows, lanes] = jnp.where(low, mixes[0], mixes[1]).astype(bf16)

    out = (wide + mm(ms[...], weight(4))).astype(bf16)
    out_wide = out.astype(f32)
    for i in range(2):
        for s2 in range(2):
            at = SEQS * i + 128 * s2
            xsc[:, i, s2, :, :E] = out_wide[at : at + 128].reshape(N, 8, E)
    out_ref[:, :I] = xsc[:, :, :, :, :E].reshape(N, I, E).astype(bf16)

    f = jnp.concatenate([f1_ref[...], f2_ref[...]], axis=0)
    factors = (mmt(f, norm(out_wide)) * alive[0:1, :]).astype(bf16)
    for i in range(2):
        r_ref[C * i : C * i + C, :] = factors[C:, SEQS * i : SEQS * i + SEQS]
    counts = [
        jnp.sum(alive[0:1, SEQS * i : SEQS * i + SEQS], axis=-1, keepdims=True)
        for i in range(2)
    ]
    row = lax.broadcasted_iota(jnp.int32, (C, SEQS), 0)
    count = jnp.where(row == 0, counts[0], counts[1]).astype(bf16)
    r_ref[2 * C :, :] = count[: RW - 2 * C, :]
    left = jnp.concatenate([factors[:C, :], count], axis=1)
    for k in range(N):
        out_ref[k, I:] = left


def column_step(me, mr, f1, f2, wo, cq, ck, cv, co, xs):
    return pl.pallas_call(
        column_kernel,
        in_specs=[pl.BlockSpec(memory_space=pltpu.SMEM)] + whole(3) + [HBM] * (5 + N),
        out_specs=whole(2),
        out_shape=[
            jax.ShapeDtypeStruct((N, 2 * I, E), bf16),
            jax.ShapeDtypeStruct((RW, SEQS), bf16),
        ],
        scratch_shapes=[
            pltpu.VMEM((2, N, 2, 8, E), f32),
            pltpu.VMEM((N, 2, 2, 8, XW), f32),
            pltpu.VMEM((ROWS, E), bf16),
            pltpu.VMEM((ROWS, E), bf16),
            pltpu.VMEM((ROWS, E), bf16),
            pltpu.VMEM((ROWS, E), bf16),
            pltpu.VMEM((5, E, E), bf16),
            pltpu.VMEM((N, I, XW), bf16),
            pltpu.SemaphoreType.DMA((5 * PARTS + N,)),
        ],
        compiler_params=params(59),
        cost_estimate=cost(5 * 2 * ROWS * E * E, 9_000_000, 2 * H * SEQS * SEQS),
    )(me, mr, f1, f2, wo, cq, ck, cv, co, *xs)


def back_kernel(in_ref, out_ref):
    o = lax.broadcasted_iota(jnp.int32, (ROWS, ROWS), 0)
    r = lax.broadcasted_iota(jnp.int32, (ROWS, ROWS), 1)
    src = (((o >> 1) & 15) << 5) + ((o & 1) << 4) + (o >> 5)
    perm = jnp.where(src == r, 1.0, 0.0).astype(bf16)
    out_ref[...] = mm(perm, in_ref[...].reshape(ROWS, E)).astype(bf16)


def back(both):
    return pl.pallas_call(
        back_kernel,
        grid=(1,),
        in_specs=[pl.BlockSpec((N, I, E), lambda n: (0, 0, 0))],
        out_specs=pl.BlockSpec((ROWS, E), lambda n: (0, 0)),
        out_shape=jax.ShapeDtypeStruct((ROWS, E), bf16),
        compiler_params=params(24),
        cost_estimate=cost(2 * ROWS * ROWS * E, 2_000_000),
    )(both)


def pair_kernel(
    me_ref, l_ref, r0, r1, r2, r3, wp_ref, out_ref,
    l0, l1, l2, l3, l4, lp, lhs, osc, wk, r_ref, n_ref,
):
    for near, ref in enumerate((r0, r1, r2, r3)):
        tail = ref[8 * C : 8 * C + 16, :128].astype(f32)
        for far in range(4):
            at = jnp.bitwise_xor(me_ref[1], 4 * far + near)
            r_ref[at] = ref[2 * C * far : 2 * C * far + 2 * C]
            n_ref[at] = tail[4 * far : 4 * far + 4]
    wk[...] = jnp.zeros_like(wk)
    for c in range(C):
        w = wp_ref[C * c : C * c + C, :]
        for j in range(4):
            at = 128 * c + C * j
            wk[at : at + C, 128 * j : 128 * j + 128] = w
    every = l_ref[...].reshape(N * C, E).astype(f32)
    for k, ref in enumerate((l0, l1, l2, l3, l4)):
        ref[...] = every[:, 128 * k : 128 * k + 128]

    def across(ref, row):
        return ref[pl.ds(row, N, stride=C), :]

    for c in range(C):
        rows = slice(C * c, C * c + C)
        lp[rows, :128] = jnp.concatenate([across(l0, c), across(l2, c)], axis=0).astype(bf16)
        lp[rows, 128:] = jnp.concatenate([across(l1, c), across(l3, c)], axis=0).astype(bf16)
    left_count = jnp.concatenate([across(l4, 0), across(l4, 1)], axis=0)
    right = r_ref[...].reshape(N * 2 * C, SEQS)
    for c in range(0, C, 4):
        outer = mmt(lp[C * c : C * c + 4 * C, :], right).astype(bf16)
        for k in range(4):
            for j in range(8):
                lhs[C * j : C * j + C, 128 * (c + k) : 128 * (c + k) + 128] = outer[
                    C * k : C * k + C, 128 * j : 128 * j + 128
                ]
    acc = mm(lhs[...], wk[...])
    right_count = n_ref[...]
    for j in range(C):
        part = acc[C * (j // 4) : C * (j // 4) + C, 128 * (j % 4) : 128 * (j % 4) + 128]
        count = right_count[j // 2, j % 2 : j % 2 + 1, :]
        part = part / (jnp.minimum(left_count, count) + 0.001)
        for i in range(2):
            osc[pl.ds(C * i + j, N, stride=2 * C), :] = part[N * i : N * i + N, :]
    out_ref[...] = osc[...].astype(bf16)


def pair_step(me, both, rights, wp):
    return pl.pallas_call(
        pair_kernel,
        grid=(1,),
        in_specs=[
            pl.BlockSpec(memory_space=pltpu.SMEM),
            pl.BlockSpec((N, I, E), lambda n: (0, 1, 0)),
        ]
        + [pl.BlockSpec((8 * C + 16, SEQS), lambda n: (0, 0))] * 4
        + [pl.BlockSpec((C * C, PC), lambda n: (0, 0))],
        out_specs=pl.BlockSpec((C * C, PC), lambda n: (0, 0)),
        out_shape=jax.ShapeDtypeStruct((C * C, PC), bf16),
        scratch_shapes=[pltpu.VMEM((N * C, 128), f32)] * 5
        + [
            pltpu.VMEM((1024, SEQS), bf16),
            pltpu.VMEM((256, 4096), bf16),
            pltpu.VMEM((1024, PC), f32),
            pltpu.VMEM((4096, 512), bf16),
            pltpu.VMEM((N, 2 * C, SEQS), bf16),
            pltpu.VMEM((N, 4, 128), f32),
        ],
        compiler_params=params(24),
        cost_estimate=cost(2 * 1024 * 1024 * 256 + 2 * 256 * 4096 * 512, 6_000_000),
    )(me, both, *rights, wp)


def exchange(x, axis):
    return lax.all_to_all(x, axis, split_axis=0, concat_axis=0, tiled=True)


def swap(x):
    pairs = [(N * d + g, N * g + d) for d in range(N) for g in range(N)]
    return lax.ppermute(x, ("depth", "cols"), pairs)


def mirror(x, k, axis):
    return lax.ppermute(x, axis, [(d, d ^ k) for d in range(N)])


def on_device(x, occupancy, wq, wk, wv, wo, cq, ck, cv, co, f1, f2, wp):
    x = x.reshape(ROWS, E)

    me = jnp.stack([lax.axis_index("depth"), lax.axis_index("cols")]).astype(jnp.int32)

    sent = row_proj(x, occupancy, wq, wk, wv)
    qkv = exchange(sent, "cols")
    later, _ = lax.optimization_barrier((x, sent))
    xs = list(turn(me, later, occupancy))
    for k in range(1, N):
        xs[k] = mirror(xs[k], k, "depth")
    qkv, xs = lax.optimization_barrier((qkv, xs))

    parts = exchange(partial_logits(qkv).reshape(N, I, SITES), "depth")
    p = exchange(row_softmax(parts), "depth")
    mix = row_mix(p, qkv)
    mr = exchange(mix.reshape(N * N, 16, 128), ("cols", "depth")).reshape(4096, 128)

    both, right = column_step(me, mr, f1.T, f2.T, wo, cq, ck, cv, co, xs)
    both = exchange(both, "depth")
    right = swap(right)
    far = [right] + [mirror(right, 4 * k, "cols") for k in range(1, 4)]
    counts = [part[2 * C : 2 * C + 4] for part in far]
    far = jnp.concatenate([part[: 2 * C] for part in far] + counts, axis=0)
    rights = [far] + [mirror(far, k, "cols") for k in range(1, 4)]
    out = back(both)
    pair = pair_step(me, both, rights, wp)
    return out.reshape(S, I, E), pair.reshape(C, C, PC)


def solution(mesh):
    placed = (P("depth", "cols", None), P("depth", "cols")) + (P(),) * 11
    return jax.shard_map(
        on_device,
        mesh=mesh,
        in_specs=placed,
        out_specs=(P("depth", "cols", None), P("cols", "depth", None)),
        check_vma=False,
    )
```
